32 devices in a mesh: ctx: 8 (over z, x), head: 4 (over y, core).
Axes of the slice: x: 2, y: 2, z: 4, core: 2. Of those that a mesh axis runs over, the one named last changes fastest.
Arguments:
- inputs: bfloat16 [1536, 2048], P('ctx'), may hold values from -6 to 6
- projection: bfloat16 [3, 2048, 1024], P(None, None, 'head'), may hold values from -0.125 to 0.125
- conv_weight: float32 [3, 4, 1024], P(None, None, 'head'), may hold values from -3 to 3
- gate_code: int32 [8, 1536], P('head', 'ctx'), may hold values from 0 to 1023
- beta_code: int32 [8, 1536], P('head', 'ctx'), may hold values from 0 to 1023
- grad_out: bfloat16 [1536, 1024], P('ctx', 'head'), may hold values from -6 to 6
Outputs:
- input_grad: bfloat16 [1536, 2048], P(('ctx', 'head'))
- kernel_grad: float32 [3, 4, 1024], P(None, None, 'head')
The draws below stay inside these ranges and needn't reach their ends.
All inputs are finite; a program needn't handle non-finite values.
Results may differ from the reference program's by a relative error of at most 0.0068.
The reference program's roundings to bfloat16 on the way (of `projected` and `rounded`) count: a program that leaves them out, or rounds other values in their place, can miss the bound.
Values may be sent and summed in bfloat16 or wider, within the bound.
A program may use at most 64 MiB of HBM per device.

```python
import jax
import jax.numpy as jnp
from jax import lax

D = 2048
H = 8
DK = 128
KW = 4
GROUP = 64
HD = 1024
TOKENS = 1536


def draw_codes(key, offset_salt, slow_level):
    ranking_key, value_key = jax.random.split(jax.random.fold_in(key, offset_salt))
    ranking = jax.random.permutation(ranking_key, H)
    levels = jnp.where(ranking < H // 2, slow_level, 1024).astype(jnp.int32)
    code_values = jax.random.randint(value_key, (H, TOKENS), 0, 1024, dtype=jnp.int32) % levels[:, None]
    code_values = code_values.at[:, 0].set(0)
    code_values = code_values.at[:, 1].set(levels - 1)
    return code_values.astype(jnp.int32)


def draw_gate_code(key, part):
    return draw_codes(key, 101, 3)


def draw_beta_code(key, part):
    return draw_codes(key, 202, 17)


def level_of(own_key, dims, cuts, least, high):
    gain = 1.0
    for axis_at, blocks in cuts:
        heights = jax.random.uniform(jax.random.fold_in(jax.random.fold_in(own_key, 6), axis_at), (blocks,), jnp.float32, least / len(cuts), high / len(cuts))
        gain = gain * jnp.repeat(jnp.exp(heights), dims[axis_at] // blocks).reshape((-1,) + (1,) * (len(dims) - 1 - axis_at))
    return gain


def bell_draw(stream_key, shape, scale, bound, cuts=(), held_as=jnp.bfloat16):
    values = jax.random.normal(stream_key, shape, jnp.float32) * scale
    if len(cuts) > 0:
        values = level_of(stream_key, shape, cuts, -0.22, 0.18) * values
    return jnp.clip(values, min=-bound, max=bound).astype(held_as)


def setup_inputs(seed: int = 0) -> dict:
    seeds = jax.random.split(jax.random.key(seed), 7)
    inputs = bell_draw(seeds[0], (TOKENS, D), 1.0, 6.0, ((0, 8),))
    projection = bell_draw(seeds[1], (3, D, HD), D ** -0.5, 0.125, ((2, 4),))
    conv_weight = bell_draw(seeds[2], (3, KW, HD), KW ** -0.5, 3.0, ((2, 4),), jnp.float32)
    gate_code = draw_gate_code(jax.random.fold_in(seeds[6], 71), 0)
    beta_code = draw_beta_code(jax.random.fold_in(seeds[6], 71), 0)
    grad_out = bell_draw(seeds[5], (TOKENS, HD), 1.0, 6.0, ((0, 8), (1, 4)))
    return {"inputs": inputs, "projection": projection, "conv_weight": conv_weight, "gate_code": gate_code, "beta_code": beta_code, "grad_out": grad_out}


HIGHEST_PRECISION = lax.Precision.HIGHEST

def normalize(matrix):
    return matrix * lax.rsqrt(lax.optimization_barrier(jnp.sum(matrix * matrix, -1, keepdims=True)) + 1e-06)

def features(extended, weights):
    length = extended.shape[1] - (KW - 1)
    convolved = weights[:, 0:1, :] * extended[:, 0:length, :]
    for offset in range(1, KW):
        convolved = convolved + weights[:, offset:offset + 1, :] * extended[:, offset:offset + length, :]
    activated = jax.nn.silu(convolved)
    head_count = activated.shape[2] // DK
    activated = activated.reshape(3, length, head_count, DK).transpose(0, 2, 1, 3)
    queries = normalize(activated[0]) * DK ** (-0.5)
    norm_keys = normalize(activated[1])
    return (queries, norm_keys, activated[2])

def block_step(carried, pieces):
    queries, norm_keys, value_rows, log_gate, beta_rate = pieces
    cumulative = jnp.cumsum(log_gate, axis=-1)
    decay_now = jnp.exp(cumulative)
    between = cumulative[:, :, None] - cumulative[:, None, :]
    position = jnp.arange(log_gate.shape[-1])
    strict = position[:, None] > position[None, :]
    inclusive = position[:, None] >= position[None, :]
    key_gram = jnp.einsum('htd,hsd->hts', norm_keys, norm_keys, precision=HIGHEST_PRECISION)
    lower_part = jnp.where(strict, jnp.exp(between), 0.0) * key_gram * beta_rate[:, :, None]
    recalled = jnp.einsum('htd,hvd->htv', norm_keys, carried, precision=HIGHEST_PRECISION)
    target = beta_rate[:, :, None] * (value_rows - decay_now[:, :, None] * recalled)
    pseudo = jax.scipy.linalg.solve_triangular(lower_part, target, lower=True, unit_diagonal=True)
    scores = jnp.einsum('htd,hsd->hts', queries, norm_keys, precision=HIGHEST_PRECISION) * jnp.where(inclusive, jnp.exp(between), 0.0)
    outputs = decay_now[:, :, None] * jnp.einsum('htd,hvd->htv', queries, carried, precision=HIGHEST_PRECISION)
    outputs = outputs + jnp.einsum('hts,hsv->htv', scores, pseudo, precision=HIGHEST_PRECISION)
    group_total = cumulative[:, -1]
    remaining = jnp.exp(group_total[:, None] - cumulative)
    new_state = jnp.exp(group_total)[:, None, None] * carried
    new_state = new_state + jnp.einsum('hsv,hsd->hvd', pseudo, remaining[:, :, None] * norm_keys, precision=HIGHEST_PRECISION)
    return (new_state, outputs)

def run_blocks(queries, norm_keys, value_rows, log_gate, beta_rate, carried):
    head_count = queries.shape[0]
    length = queries.shape[1]
    blocks = length // GROUP

    def to_blocks(tensor):
        return jnp.moveaxis(tensor.reshape((tensor.shape[0], blocks, GROUP) + tensor.shape[2:]), 1, 0)
    final_state, outputs = lax.scan(jax.checkpoint(block_step), carried, (to_blocks(queries), to_blocks(norm_keys), to_blocks(value_rows), to_blocks(log_gate), to_blocks(beta_rate)))
    outputs = jnp.moveaxis(outputs, 0, 1).reshape(head_count, length, DK)
    return (outputs, final_state)

def reference(inputs, projection, conv_weight, gate_code, beta_code, grad_out):
    projected = jnp.stack([jnp.dot(inputs.astype(jnp.float32), projection[member].astype(jnp.float32), preferred_element_type=jnp.float32) for member in range(3)]).astype(jnp.bfloat16)
    log_gate = jnp.log(1.0 - 0.001 * gate_code.astype(jnp.float32) / 1023.0)
    beta_rate = beta_code.astype(jnp.float32) / 1023.0

    def forward(raw_float, weights):
        extended = jnp.pad(raw_float, ((0, 0), (KW - 1, 0), (0, 0)))
        queries, norm_keys, value_rows = features(extended, weights)
        outputs, final_state = run_blocks(queries, norm_keys, value_rows, log_gate, beta_rate, jnp.zeros((H, DK, DK), jnp.float32))
        return outputs
    primal, pullback = jax.vjp(forward, projected.astype(jnp.float32), conv_weight)
    cotangent = grad_out.astype(jnp.float32).reshape(TOKENS, H, DK).transpose(1, 0, 2)
    raw_grad, weight_grad = pullback(cotangent)
    rounded = raw_grad.astype(jnp.bfloat16)
    input_grad = jnp.einsum('mtc,mdc->td', rounded.astype(jnp.float32), projection.astype(jnp.float32), preferred_element_type=jnp.float32)
    return (input_grad.astype(jnp.bfloat16), weight_grad)
```

```python
import functools

import jax
import jax.numpy as jnp
from jax import lax
from jax.experimental import pallas as pl
from jax.experimental.pallas import tpu as pltpu
from jax.sharding import PartitionSpec as P

DK = 128
KW = 4
HALO = 16
F32 = jnp.float32
BF16 = jnp.bfloat16
VMEM = pl.BlockSpec(memory_space=pltpu.VMEM)


def contract(a, b, dims, precise):
    if precise:
        return lax.dot_general(
            a, b, (dims, ((), ())), precision=lax.Precision.HIGHEST, preferred_element_type=F32
        )
    return lax.dot_general(
        a.astype(BF16), b.astype(BF16), (dims, ((), ())), preferred_element_type=F32
    )


def nn(a, b, precise=False):
    return contract(a, b, ((1,), (0,)), precise)


def nt(a, b, precise=False):
    return contract(a, b, ((1,), (1,)), precise)


def tn(a, b, precise=False):
    return contract(a, b, ((0,), (0,)), precise)


def unit_inverses(lowers, eye, distance):
    count = eye.shape[0]
    inverses = [eye - jnp.where(distance == 1, low, 0.0) for low in lowers]
    size = 2
    while size < count:
        mask = (distance >= size) & (distance < 2 * size)
        inner = [nn(inv, jnp.where(mask, low, 0.0)) for inv, low in zip(inverses, lowers)]
        inverses = [inv - nn(mid, inv) for inv, mid in zip(inverses, inner)]
        size *= 2
    left = [eye - inv - nn(low, inv, True) for inv, low in zip(inverses, lowers)]
    return [inv + nn(inv, rest) for inv, rest in zip(inverses, left)]


def local_part(tail, x_ref, w_ref, cw_ref, gate_ref, beta_ref, g_ref, ext, heads):
    count = x_ref.shape[0]
    for m in range(3):
        weights = w_ref[m]
        ext[m, HALO:, :] = nn(x_ref[...], weights).astype(BF16).astype(F32)
        ext[m, :HALO, :] = nn(tail, weights).astype(BF16).astype(F32)
    rows = lax.broadcasted_iota(jnp.int32, (count, count), 0)
    cols = lax.broadcasted_iota(jnp.int32, (count, count), 1)
    eye = (rows == cols).astype(F32)
    inclusive = (rows >= cols).astype(F32)
    strict = (rows > cols).astype(F32)
    log_gate = jnp.log(1.0 - 0.001 * gate_ref[...].astype(F32) / 1023.0)
    beta_rows = beta_ref[...].astype(F32) / 1023.0
    sums_row = nt(log_gate, inclusive, True)
    sums_col = nt(inclusive, log_gate, True)
    beta_cols = nt(eye, beta_rows, True)
    act = []
    for m in range(3):
        conv = cw_ref[m, 0:1, :] * ext[m, HALO - 3 : HALO - 3 + count, :]
        for j in range(1, KW):
            conv = conv + cw_ref[m, j : j + 1, :] * ext[m, HALO - 3 + j : HALO - 3 + j + count, :]
        sig = jax.nn.sigmoid(conv)
        act.append((conv * sig, sig * (1.0 + conv * (1.0 - sig))))
    out = []
    for h in range(heads):
        lanes = slice(h * DK, (h + 1) * DK)
        q_act, k_act, v = (act[m][0][:, lanes] for m in range(3))
        q_scale = lax.rsqrt(jnp.sum(q_act * q_act, -1, keepdims=True) + 1e-6)
        k_scale = lax.rsqrt(jnp.sum(k_act * k_act, -1, keepdims=True) + 1e-6)
        qn = q_act * q_scale
        s_col = sums_col[:, h : h + 1]
        beta = beta_cols[:, h : h + 1]
        total = s_col[count - 1 : count, :]
        d = dict(
            q=qn * DK**-0.5,
            k=k_act * k_scale,
            v=v,
            q_scale=q_scale * DK**-0.5,
            k_scale=k_scale,
            qn=qn,
            beta=beta,
            now=jnp.exp(s_col),
            rest=jnp.exp(total - s_col),
            whole=jnp.exp(total),
            g=g_ref[:, lanes].astype(F32),
            between=jnp.exp(s_col - sums_row[h : h + 1, :]),
        )
        d["low_scale"] = d["between"] * strict * beta
        d["between"] = d["between"] * inclusive
        out.append(d)
    for d in out:
        d["low"] = nt(d["k"], d["k"], True) * d["low_scale"]
    inverses = unit_inverses([d["low"] for d in out], eye, rows ^ cols)
    for d, inv in zip(out, inverses):
        d["inv"] = inv
        d["scores"] = nt(d["q"], d["k"]) * d["between"]
        d["k_rest"] = d["rest"] * d["k"]
        d["k_now"] = (d["beta"] * d["now"]) * d["k"]
        solved = nn(inv, jnp.concatenate([d["beta"] * d["v"], d["k_now"]], 1), True)
        d["u0"] = solved[:, :DK]
        d["kt"] = solved[:, DK:]
        both = tn(solved, d["k_rest"], True)
        d["B"] = both[:DK]
        d["A"] = d["whole"] * eye[:DK, :DK] - both[DK:]
        d["wg"] = tn(d["scores"], d["g"])
        d["C"] = tn(d["g"], d["now"] * d["q"]) - tn(d["wg"], d["kt"])
    return act, out


def carried_part(act, per_head, cw_ref, ext, grads, states):
    count = grads.shape[1] - 8
    parts = [[], [], []]
    for d, (start, arriving) in zip(per_head, states):
        u = d["u0"] - nt(d["kt"], start)
        du = d["wg"] + nt(d["k_rest"], arriving)
        y = tn(d["inv"], du)
        yg = jnp.concatenate([y, d["g"]], 0)
        outer = nt(yg, u)
        through = nn(yg, start)
        lows = jnp.concatenate(
            [-d["low_scale"] * outer[:count], d["between"] * outer[count:]], 0
        )
        by_rows = nn(lows, d["k"])
        by_cols = tn(lows, jnp.concatenate([d["k"], d["q"]], 0))
        dq = d["now"] * through[count:] + by_rows[count:]
        dk = (
            by_rows[:count]
            + by_cols
            - (d["beta"] * d["now"]) * through[:count]
            + d["rest"] * nn(u, arriving)
        )
        dq = d["q_scale"] * (dq - d["qn"] * jnp.sum(d["qn"] * dq, -1, keepdims=True))
        dk = d["k_scale"] * (dk - d["k"] * jnp.sum(d["k"] * dk, -1, keepdims=True))
        for m, part in enumerate((dq, dk, d["beta"] * y)):
            parts[m].append(part)
    tap_rows = []
    for m in range(3):
        dconv = jnp.concatenate(parts[m], 1) * act[m][1]
        grads[m, :count, :] = dconv
        for j in range(KW):
            tap_rows.append(
                jnp.sum(
                    dconv * ext[m, HALO - 3 + j : HALO - 3 + j + count, :], 0, keepdims=True
                )
            )
    return tap_rows


def raw_part(cw_ref, grads, m, count):
    raw = cw_ref[m, KW - 1 : KW, :] * grads[m, 0:count, :]
    for j in range(KW - 1):
        raw = raw + cw_ref[m, j : j + 1, :] * grads[m, KW - 1 - j : KW - 1 - j + count, :]
    return raw.astype(BF16)


def scan_states(get, me, ctx, heads):
    zero = jnp.zeros((DK, DK), F32)

    def step(i, carry):
        new = []
        back = ctx - 1 - i
        for h in range(heads):
            start, arriving = carry[h]
            keep_start = jnp.where(i < me, 1.0, 0.0)
            keep_back = jnp.where(back > me, 1.0, 0.0)
            start_next = nn(start, get(i, h, 0), True) + get(i, h, 1)
            back_next = nt(arriving, get(back, h, 0), True) + get(back, h, 2)
            new.append(
                (
                    keep_start * start_next + (1.0 - keep_start) * start,
                    keep_back * back_next + (1.0 - keep_back) * arriving,
                )
            )
        return tuple(new)

    return lax.fori_loop(0, ctx - 1, step, tuple((zero, zero) for _ in range(heads)))


def first_kernel(heads, tail, x, w, cw, gate, beta, g, mats, ext):
    _, out = local_part(tail[...], x, w, cw, gate, beta, g, ext, heads)
    for h, d in enumerate(out):
        for i, name in enumerate("ABC"):
            mats[h, i] = d[name]


def second_kernel(heads, ctx, tail, x, w, cw, gate, beta, g, mats, dconv, taps, ext, grads):
    me = lax.axis_index("ctx")
    act, out = local_part(tail[...], x, w, cw, gate, beta, g, ext, heads)
    states = scan_states(lambda i, h, n: mats[i, h, n], me, ctx, heads)
    tap_rows = carried_part(act, out, cw, ext, grads, states)
    for n, row in enumerate(tap_rows):
        taps[n : n + 1, :] = row
    dconv[...] = grads[:, : x.shape[0], :]


def third_kernel(w, cw, dconv, spill, out, grads):
    count = dconv.shape[1]
    grads[:, :count, :] = dconv[...]
    grads[:, count:, :] = spill[...]
    total = nt(raw_part(cw, grads, 0, count), w[0])
    for m in (1, 2):
        total = total + nt(raw_part(cw, grads, m, count), w[m])
    out[...] = total


def from_behind(block, axis, distance):
    devices = range(lax.axis_size(axis))
    route = [(i - distance, i) for i in devices if i - distance in devices]
    return lax.ppermute(block, axis, route)


def on_device(inputs, projection, conv_weight, gate_code, beta_code, grad_out):
    count = inputs.shape[0]
    heads = gate_code.shape[0]
    width = heads * DK
    ctx = lax.axis_size("ctx")
    params = pltpu.CompilerParams(vmem_limit_bytes=56 * 1024 * 1024)
    tail = from_behind(inputs[count - HALO :], "ctx", 1)
    ext = pltpu.VMEM((3, count + HALO, width), F32)
    grads = pltpu.VMEM((3, count + 8, width), F32)
    mats = pl.pallas_call(
        functools.partial(first_kernel, heads),
        out_shape=jax.ShapeDtypeStruct((heads, 3, DK, DK), F32),
        in_specs=[VMEM] * 7,
        out_specs=VMEM,
        scratch_shapes=[ext],
        compiler_params=params,
    )(tail, inputs, projection, conv_weight, gate_code, beta_code, grad_out)
    gathered = lax.all_gather(mats, "ctx")
    dconv, taps = pl.pallas_call(
        functools.partial(second_kernel, heads, ctx),
        out_shape=(
            jax.ShapeDtypeStruct((3, count, width), F32),
            jax.ShapeDtypeStruct((3 * KW, width), F32),
        ),
        in_specs=[VMEM] * 8,
        out_specs=(VMEM, VMEM),
        scratch_shapes=[ext, grads],
        compiler_params=params,
    )(tail, inputs, projection, conv_weight, gate_code, beta_code, grad_out, gathered)
    spill = from_behind(dconv[:, :8, :], "ctx", -1)
    partial = pl.pallas_call(
        third_kernel,
        out_shape=jax.ShapeDtypeStruct(inputs.shape, F32),
        in_specs=[VMEM] * 4,
        out_specs=VMEM,
        scratch_shapes=[grads],
        compiler_params=params,
    )(projection, conv_weight, dconv, spill)
    input_grad = lax.psum_scatter(partial, "head", scatter_dimension=0, tiled=True)
    kernel_grad = lax.psum(taps.reshape(3, KW, width), "ctx")
    return (input_grad.astype(BF16), kernel_grad)


def solution(mesh):
    return jax.shard_map(
        on_device,
        mesh=mesh,
        in_specs=(
            P("ctx", None),
            P(None, None, "head"),
            P(None, None, "head"),
            P("head", "ctx"),
            P("head", "ctx"),
            P("ctx", "head"),
        ),
        out_specs=(P(("ctx", "head"), None), P(None, None, "head")),
        check_vma=False,
    )
```

```python
import functools

import jax
import jax.numpy as jnp
from jax import lax
from jax.experimental import pallas as pl
from jax.experimental.pallas import tpu as pltpu
from jax.sharding import PartitionSpec as P

DK = 128
KW = 4
HALO = 16
F32 = jnp.float32
BF16 = jnp.bfloat16
VMEM = pl.BlockSpec(memory_space=pltpu.VMEM)


def contract(a, b, dims, precise):
    def one(left, right):
        return lax.dot_general(left, right, (dims, ((), ())), preferred_element_type=F32)

    if not precise:
        return one(a.astype(BF16), b.astype(BF16))
    a_high, b_high = a.astype(BF16), b.astype(BF16)
    total = one(a_high, b_high)
    if b.dtype == F32:
        total = total + one(a_high, (b - b_high.astype(F32)).astype(BF16))
    if a.dtype == F32:
        total = total + one((a - a_high.astype(F32)).astype(BF16), b_high)
    return total


def exact_nt(a, b):
    return lax.dot_general(
        a, b, (((1,), (1,)), ((), ())), precision=lax.Precision.HIGHEST, preferred_element_type=F32
    )


def nn(a, b, precise=False):
    return contract(a, b, ((1,), (0,)), precise)


def nt(a, b, precise=False):
    return contract(a, b, ((1,), (1,)), precise)


def tn(a, b, precise=False):
    return contract(a, b, ((0,), (0,)), precise)


def unit_inverses(lowers, eye, distance):
    count = eye.shape[0]
    inverses = [eye - jnp.where(distance == 1, low, 0.0) for low in lowers]
    size = 2
    while size < count:
        mask = (distance >= size) & (distance < 2 * size)
        inner = [nn(inv, jnp.where(mask, low, 0.0)) for inv, low in zip(inverses, lowers)]
        inverses = [inv - nn(mid, inv) for inv, mid in zip(inverses, inner)]
        size *= 2
    left = [eye - inv - nn(low, inv, True) for inv, low in zip(inverses, lowers)]
    return [inv + nn(inv, rest) for inv, rest in zip(inverses, left)]


def local_part(get_tail, x_ref, w_ref, cw_ref, gate_ref, beta_ref, g_ref, ext, heads):
    count = x_ref.shape[0]
    for m in range(3):
        ext[m, HALO:, :] = nn(x_ref[...], w_ref[m]).astype(BF16).astype(F32)
    tail = get_tail()
    for m in range(3):
        ext[m, :HALO, :] = nn(tail, w_ref[m]).astype(BF16).astype(F32)
    rows = lax.broadcasted_iota(jnp.int32, (count, count), 0)
    cols = lax.broadcasted_iota(jnp.int32, (count, count), 1)
    eye = (rows == cols).astype(F32)
    inclusive = (rows >= cols).astype(F32)
    strict = (rows > cols).astype(F32)
    log_gate = jnp.log(1.0 - 0.001 * gate_ref[...].astype(F32) / 1023.0)
    beta_rows = beta_ref[...].astype(F32) / 1023.0
    sums_row = exact_nt(log_gate, inclusive)
    sums_col = exact_nt(inclusive, log_gate)
    beta_cols = exact_nt(eye, beta_rows)
    act = []
    for m in range(3):
        conv = cw_ref[m, 0:1, :] * ext[m, HALO - 3 : HALO - 3 + count, :]
        for j in range(1, KW):
            conv = conv + cw_ref[m, j : j + 1, :] * ext[m, HALO - 3 + j : HALO - 3 + j + count, :]
        sig = jax.nn.sigmoid(conv)
        act.append((conv * sig, sig * (1.0 + conv * (1.0 - sig))))
    out = []
    for h in range(heads):
        lanes = slice(h * DK, (h + 1) * DK)
        q_act, k_act, v = (act[m][0][:, lanes] for m in range(3))
        q_scale = lax.rsqrt(jnp.sum(q_act * q_act, -1, keepdims=True) + 1e-6)
        k_scale = lax.rsqrt(jnp.sum(k_act * k_act, -1, keepdims=True) + 1e-6)
        qn = q_act * q_scale
        s_col = sums_col[:, h : h + 1]
        beta = beta_cols[:, h : h + 1]
        total = s_col[count - 1 : count, :]
        d = dict(
            q=qn * DK**-0.5,
            k=k_act * k_scale,
            v=v,
            q_scale=q_scale * DK**-0.5,
            k_scale=k_scale,
            qn=qn,
            beta=beta,
            now=jnp.exp(s_col),
            rest=jnp.exp(total - s_col),
            whole=jnp.exp(total),
            g=g_ref[:, lanes],
            between=jnp.exp(s_col - sums_row[h : h + 1, :]),
        )
        d["low_scale"] = d["between"] * strict * beta
        d["between"] = d["between"] * inclusive
        out.append(d)
    for d in out:
        d["low"] = nt(d["k"], d["k"], True) * d["low_scale"]
    inverses = unit_inverses([d["low"] for d in out], eye, rows ^ cols)
    for d, inv in zip(out, inverses):
        d["inv"] = inv
        d["scores"] = nt(d["q"], d["k"], True) * d["between"]
        d["k_rest"] = d["rest"] * d["k"]
        d["k_now"] = (d["beta"] * d["now"]) * d["k"]
        solved = nn(inv, jnp.concatenate([d["beta"] * d["v"], d["k_now"]], 1), True)
        d["u0"] = solved[:, :DK]
        d["kt"] = solved[:, DK:]
        both = tn(solved, d["k_rest"], True)
        d["B"] = both[:DK]
        d["A"] = d["whole"] * eye[:DK, :DK] - both[DK:]
        d["wg"] = tn(d["scores"], d["g"], True)
        d["C"] = tn(d["g"], d["now"] * d["q"], True) - tn(d["wg"], d["kt"], True)
    return act, out


def carried_part(act, per_head, cw_ref, ext, grads, states):
    count = grads.shape[1] - 8
    parts = [[], [], []]
    for d, (start, arriving) in zip(per_head, states):
        u = d["u0"] - nt(d["kt"], start, True)
        du = d["wg"] + nt(d["k_rest"], arriving, True)
        y = tn(d["inv"], du, True)
        yg = jnp.concatenate([y.astype(BF16), d["g"]], 0)
        outer = nt(yg, u)
        through = nn(yg, start)
        lows = jnp.concatenate(
            [-d["low_scale"] * outer[:count], d["between"] * outer[count:]], 0
        )
        by_rows = nn(lows, d["k"])
        by_cols = tn(lows, jnp.concatenate([d["k"], d["q"]], 0))
        dq = d["now"] * through[count:] + by_rows[count:]
        dk = (
            by_rows[:count]
            + by_cols
            - (d["beta"] * d["now"]) * through[:count]
            + d["rest"] * nn(u, arriving)
        )
        dq = d["q_scale"] * (dq - d["qn"] * jnp.sum(d["qn"] * dq, -1, keepdims=True))
        dk = d["k_scale"] * (dk - d["k"] * jnp.sum(d["k"] * dk, -1, keepdims=True))
        for m, part in enumerate((dq, dk, d["beta"] * y)):
            parts[m].append(part)
    for m in range(3):
        grads[m, :count, :] = jnp.concatenate(parts[m], 1) * act[m][1]


def tap_sums(ext, grads, taps):
    count = grads.shape[1] - 8
    for m in range(3):
        dconv = grads[m, :count, :]
        for j in range(KW):
            row = m * KW + j
            taps[row : row + 1, :] = jnp.sum(
                dconv * ext[m, HALO - 3 + j : HALO - 3 + j + count, :], 0, keepdims=True
            )
    taps[3 * KW :, :] = jnp.zeros((16 - 3 * KW, taps.shape[1]), F32)


def raw_part(cw_ref, grads, m, count):
    raw = cw_ref[m, KW - 1 : KW, :] * grads[m, 0:count, :]
    for j in range(KW - 1):
        raw = raw + cw_ref[m, j : j + 1, :] * grads[m, KW - 1 - j : KW - 1 - j + count, :]
    return raw.astype(BF16)


def whole_kernel(
    heads,
    x,
    w,
    cw,
    gate,
    beta,
    g,
    out,
    taps_out,
    ext,
    grads,
    tail,
    spill,
    pair_out,
    pair_in,
    chain_out,
    chain_in,
    taps,
    rounded,
    partial_out,
    partial_in,
    tail_sems,
    spill_sems,
    pair_sems,
    chain_send,
    chain_recv,
    taps_send,
    taps_recv,
    partial_send,
    partial_recv,
):
    count, depth = x.shape
    ctx, head_axis = lax.axis_size("ctx"), lax.axis_size("head")
    me, head_me = lax.axis_index("ctx"), lax.axis_index("head")
    pairs = ctx // 2
    place, odd = me // 2, me % 2

    def send(src, dst, send_sem, recv_sem, axis, target):
        return pltpu.make_async_remote_copy(
            src_ref=src,
            dst_ref=dst,
            send_sem=send_sem,
            recv_sem=recv_sem,
            device_id={axis: target},
            device_id_type=pl.DeviceIdType.MESH,
        )

    barrier = pltpu.get_barrier_semaphore()
    for axis, at, size in (("ctx", me, ctx), ("head", head_me, head_axis)):
        for d in range(1, size):
            pl.semaphore_signal(
                barrier,
                inc=1,
                device_id={axis: (at + d) % size},
                device_id_type=pl.DeviceIdType.MESH,
            )
    pl.semaphore_wait(barrier, ctx + head_axis - 2)

    tail_copy = send(
        x.at[count - HALO :], tail, tail_sems.at[0], tail_sems.at[1], "ctx", (me + 1) % ctx
    )
    tail_copy.start()

    def get_tail():
        tail_copy.wait()
        return jnp.where(me == 0, jnp.zeros_like(tail), tail[...])

    act, per_head = local_part(get_tail, x, w, cw, gate, beta, g, ext, heads)
    for h, d in enumerate(per_head):
        for i, name in enumerate("ABC"):
            pair_out[h, i] = d[name].astype(BF16)
    pair_copy = send(
        pair_out, pair_in, pair_sems.at[0], pair_sems.at[1], "ctx", me + 1 - 2 * odd
    )
    pair_copy.start()
    pair_copy.wait()
    is_odd = odd == 1
    early, late, merged = [], [], []
    for h, d in enumerate(per_head):
        own = [d[name] for name in "ABC"]
        other = [pair_in[h, i].astype(F32) for i in range(3)]
        first = [jnp.where(is_odd, o, m) for m, o in zip(own, other)]
        second = [jnp.where(is_odd, m, o) for m, o in zip(own, other)]
        early.append(first)
        late.append(second)
        merged.append(
            (
                nn(first[0], second[0], True),
                nn(first[1], second[0], True) + second[1],
                nt(second[2], first[0], True) + first[2],
            )
        )

    forward_copy = send(
        chain_out.at[0], chain_in.at[0], chain_send.at[0], chain_recv.at[0], "ctx", (me + 2) % ctx
    )
    backward_copy = send(
        chain_out.at[1],
        chain_in.at[1],
        chain_send.at[1],
        chain_recv.at[1],
        "ctx",
        (me + ctx - 2) % ctx,
    )

    def forward():
        @pl.when(place == 0)
        def _():
            chain_in[0] = jnp.zeros_like(chain_in[0])

        @pl.when(place > 0)
        def _():
            forward_copy.wait_recv()

        @pl.when(place < pairs - 1)
        def _():
            for h in range(heads):
                chain_out[0, h] = (
                    nn(chain_in[0, h], merged[h][0], True) + merged[h][1]
                ).astype(BF16)
            forward_copy.start()

    def backward():
        @pl.when(place == pairs - 1)
        def _():
            chain_in[1] = jnp.zeros_like(chain_in[1])

        @pl.when(place < pairs - 1)
        def _():
            backward_copy.wait_recv()

        @pl.when(place > 0)
        def _():
            for h in range(heads):
                chain_out[1, h] = (
                    nt(chain_in[1, h], merged[h][0], True) + merged[h][2]
                ).astype(BF16)
            backward_copy.start()

    @pl.when(place < pairs // 2)
    def _():
        forward()
        backward()

    @pl.when(place >= pairs // 2)
    def _():
        backward()
        forward()

    states = []
    for h in range(heads):
        start, arriving = chain_in[0, h], chain_in[1, h]
        start_odd = nn(start, early[h][0], True) + early[h][1]
        arriving_even = nt(arriving, late[h][0], True) + late[h][2]
        states.append(
            (
                jnp.where(is_odd, start_odd, start.astype(F32)),
                jnp.where(is_odd, arriving.astype(F32), arriving_even),
            )
        )
    carried_part(act, per_head, cw, ext, grads, states)
    spill_copy = send(
        grads.at[:, 0:8, :], spill, spill_sems.at[0], spill_sems.at[1], "ctx", (me + ctx - 1) % ctx
    )
    spill_copy.start()
    tap_sums(ext, grads, taps.at[me])
    taps_copies = [
        send(
            taps.at[me],
            taps.at[me],
            taps_send.at[d - 1],
            taps_recv.at[d - 1],
            "ctx",
            (me + d) % ctx,
        )
        for d in range(1, ctx)
    ]
    for copy in taps_copies:
        copy.start()
    spill_copy.wait()
    grads[:, count:, :] = jnp.where(me == ctx - 1, jnp.zeros_like(spill), spill[...])
    width = w.shape[2]
    for m in range(3):
        rounded[:, m * width : (m + 1) * width] = raw_part(cw, grads, m, count)
    block = count // head_axis
    chunks, _, span = partial_out.shape
    own = []
    copies = []
    for c in range(chunks):
        total = None
        for m in range(3):
            term = nt(
                rounded[:, m * width : (m + 1) * width], w[m, c * span : (c + 1) * span, :]
            )
            total = term if total is None else total + term
        partial_out[c] = total.astype(BF16)
        for d in (2, 1, 3) if head_axis == 4 else range(1, head_axis):
            target = (head_me + d) % head_axis
            copy = send(
                partial_out.at[c, pl.ds(pl.multiple_of(target * block, 16), block)],
                partial_in.at[d - 1, c],
                partial_send.at[d - 1, c],
                partial_recv.at[d - 1, c],
                "head",
                target,
            )
            copy.start()
            copies.append(copy)
    for copy in taps_copies:
        copy.wait()
    summed = taps[0]
    for i in range(1, ctx):
        summed = summed + taps[i]
    taps_out[...] = summed[: 3 * KW]
    for copy in copies:
        copy.wait()
    for c in range(chunks):
        total = partial_out[c, pl.ds(pl.multiple_of(head_me * block, 16), block), :].astype(F32)
        for d in range(1, head_axis):
            total = total + partial_in[d - 1, c].astype(F32)
        out[:, c * span : (c + 1) * span] = total.astype(BF16)

    @pl.when(place < pairs - 1)
    def _():
        forward_copy.wait_send()

    @pl.when(place > 0)
    def _():
        backward_copy.wait_send()


def on_device(inputs, projection, conv_weight, gate_code, beta_code, grad_out):
    count, depth = inputs.shape
    heads = gate_code.shape[0]
    width = heads * DK
    ctx, head_axis = lax.axis_size("ctx"), lax.axis_size("head")
    chunks = 4
    span = depth // chunks
    block = count // head_axis
    dma = pltpu.SemaphoreType.DMA
    input_grad, taps = pl.pallas_call(
        functools.partial(whole_kernel, heads),
        out_shape=(
            jax.ShapeDtypeStruct((block, depth), BF16),
            jax.ShapeDtypeStruct((3 * KW, width), F32),
        ),
        in_specs=[VMEM] * 6,
        out_specs=(VMEM, VMEM),
        scratch_shapes=[
            pltpu.VMEM((3, count + HALO, width), F32),
            pltpu.VMEM((3, count + 8, width), F32),
            pltpu.VMEM((HALO, depth), BF16),
            pltpu.VMEM((3, 8, width), F32),
            pltpu.VMEM((heads, 3, DK, DK), BF16),
            pltpu.VMEM((heads, 3, DK, DK), BF16),
            pltpu.VMEM((2, heads, DK, DK), BF16),
            pltpu.VMEM((2, heads, DK, DK), BF16),
            pltpu.VMEM((ctx, 16, width), F32),
            pltpu.VMEM((count, 3 * width), BF16),
            pltpu.VMEM((chunks, count, span), BF16),
            pltpu.VMEM((head_axis - 1, chunks, block, span), BF16),
            dma((2,)),
            dma((2,)),
            dma((2,)),
            dma((2,)),
            dma((2,)),
            dma((ctx - 1,)),
            dma((ctx - 1,)),
            dma((head_axis - 1, chunks)),
            dma((head_axis - 1, chunks)),
        ],
        compiler_params=pltpu.CompilerParams(
            collective_id=0, has_side_effects=True, vmem_limit_bytes=56 * 1024 * 1024
        ),
    )(inputs, projection, conv_weight, gate_code, beta_code, grad_out)
    return (input_grad, taps.reshape(3, KW, width))


def solution(mesh):
    return jax.shard_map(
        on_device,
        mesh=mesh,
        in_specs=(
            P("ctx", None),
            P(None, None, "head"),
            P(None, None, "head"),
            P("head", "ctx"),
            P("head", "ctx"),
            P("ctx", "head"),
        ),
        out_specs=(P(("ctx", "head"), None), P(None, None, "head")),
        check_vma=False,
    )
```

```python
import functools

import jax
import jax.numpy as jnp
from jax import lax
from jax.experimental import pallas as pl
from jax.experimental.pallas import tpu as pltpu
from jax.sharding import PartitionSpec as P

DK = 128
KW = 4
HALO = 16
F32 = jnp.float32
BF16 = jnp.bfloat16
VMEM = pl.BlockSpec(memory_space=pltpu.VMEM)
ANY = pl.BlockSpec(memory_space=pl.ANY)


def contract(a, b, dims, precise):
    def one(left, right):
        return lax.dot_general(left, right, (dims, ((), ())), preferred_element_type=F32)

    if not precise:
        return one(a.astype(BF16), b.astype(BF16))
    a_high, b_high = a.astype(BF16), b.astype(BF16)
    total = one(a_high, b_high)
    if b.dtype == F32:
        total = total + one(a_high, (b - b_high.astype(F32)).astype(BF16))
    if a.dtype == F32:
        total = total + one((a - a_high.astype(F32)).astype(BF16), b_high)
    return total


def exact_nt(a, b):
    return lax.dot_general(
        a, b, (((1,), (1,)), ((), ())), precision=lax.Precision.HIGHEST, preferred_element_type=F32
    )


def nn(a, b, precise=False):
    return contract(a, b, ((1,), (0,)), precise)


def nt(a, b, precise=False):
    return contract(a, b, ((1,), (1,)), precise)


def tn(a, b, precise=False):
    return contract(a, b, ((0,), (0,)), precise)


def unit_inverses(lowers, eye, distance):
    count = eye.shape[0]
    inverses = [eye - jnp.where(distance == 1, low, 0.0) for low in lowers]
    size = 2
    while size < count:
        mask = (distance >= size) & (distance < 2 * size)
        inner = [nn(inv, jnp.where(mask, low, 0.0)) for inv, low in zip(inverses, lowers)]
        inverses = [inv - nn(mid, inv) for inv, mid in zip(inverses, inner)]
        size *= 2
    left = [eye - inv - nn(low, inv, True) for inv, low in zip(inverses, lowers)]
    return [inv + nn(inv, rest) for inv, rest in zip(inverses, left)]


def local_part(get_weights, get_tail, x_ref, w_ref, cw_ref, gate_ref, beta_ref, g_ref, ext, heads):
    count = x_ref.shape[0]
    for m in (1, 0, 2):
        get_weights(m)
        ext[m, HALO:, :] = nn(x_ref[...], w_ref[m]).astype(BF16).astype(F32)
    tail = get_tail()
    for m in range(3):
        ext[m, :HALO, :] = nn(tail, w_ref[m]).astype(BF16).astype(F32)
    rows = lax.broadcasted_iota(jnp.int32, (count, count), 0)
    cols = lax.broadcasted_iota(jnp.int32, (count, count), 1)
    eye = (rows == cols).astype(F32)
    inclusive = (rows >= cols).astype(F32)
    strict = (rows > cols).astype(F32)
    log_gate = jnp.log(1.0 - 0.001 * gate_ref[...].astype(F32) / 1023.0)
    beta_rows = beta_ref[...].astype(F32) / 1023.0
    sums_row = exact_nt(log_gate, inclusive)
    sums_col = exact_nt(inclusive, log_gate)
    beta_cols = exact_nt(eye, beta_rows)
    act = []
    for m in range(3):
        conv = cw_ref[m, 0:1, :] * ext[m, HALO - 3 : HALO - 3 + count, :]
        for j in range(1, KW):
            conv = conv + cw_ref[m, j : j + 1, :] * ext[m, HALO - 3 + j : HALO - 3 + j + count, :]
        sig = jax.nn.sigmoid(conv)
        act.append((conv * sig, sig * (1.0 + conv * (1.0 - sig))))
    out = []
    for h in range(heads):
        lanes = slice(h * DK, (h + 1) * DK)
        q_act, k_act, v = (act[m][0][:, lanes] for m in range(3))
        q_scale = lax.rsqrt(jnp.sum(q_act * q_act, -1, keepdims=True) + 1e-6)
        k_scale = lax.rsqrt(jnp.sum(k_act * k_act, -1, keepdims=True) + 1e-6)
        qn = q_act * q_scale
        s_col = sums_col[:, h : h + 1]
        beta = beta_cols[:, h : h + 1]
        total = s_col[count - 1 : count, :]
        d = dict(
            q=qn * DK**-0.5,
            k=k_act * k_scale,
            v=v,
            q_scale=q_scale * DK**-0.5,
            k_scale=k_scale,
            qn=qn,
            beta=beta,
            now=jnp.exp(s_col),
            rest=jnp.exp(total - s_col),
            whole=jnp.exp(total),
            g=g_ref[:, lanes],
            between=jnp.exp(s_col - sums_row[h : h + 1, :]),
        )
        d["low_scale"] = d["between"] * strict * beta
        d["between"] = d["between"] * inclusive
        out.append(d)
    for d in out:
        d["low"] = nt(d["k"], d["k"], True) * d["low_scale"]
    inverses = unit_inverses([d["low"] for d in out], eye, rows ^ cols)
    for d, inv in zip(out, inverses):
        d["inv"] = inv
        d["scores"] = nt(d["q"], d["k"], True) * d["between"]
        d["k_rest"] = d["rest"] * d["k"]
        d["k_now"] = (d["beta"] * d["now"]) * d["k"]
        solved = nn(inv, jnp.concatenate([d["beta"] * d["v"], d["k_now"]], 1), True)
        d["u0"] = solved[:, :DK]
        d["kt"] = solved[:, DK:]
        both = tn(solved, d["k_rest"], True)
        d["B"] = both[:DK]
        d["A"] = d["whole"] * eye[:DK, :DK] - both[DK:]
        d["wg"] = tn(d["scores"], d["g"], True)
        d["C"] = tn(d["g"], d["now"] * d["q"], True) - tn(d["wg"], d["kt"], True)
    return act, out


def carried_part(act, per_head, cw_ref, ext, grads, states):
    count = grads.shape[1] - 8
    parts = [[], [], []]
    for d, (start, arriving) in zip(per_head, states):
        u = d["u0"] - nt(d["kt"], start, True)
        y = d["y0"] + nt(d["kt_rest"], arriving, True)
        yg = jnp.concatenate([y.astype(BF16), d["g"]], 0)
        outer = nt(yg, u)
        through = nn(yg, start)
        lows = jnp.concatenate(
            [-d["low_scale"] * outer[:count], d["between"] * outer[count:]], 0
        )
        by_rows = nn(lows, d["k"])
        by_cols = tn(lows, jnp.concatenate([d["k"], d["q"]], 0))
        dq = d["now"] * through[count:] + by_rows[count:]
        dk = (
            by_rows[:count]
            + by_cols
            - (d["beta"] * d["now"]) * through[:count]
            + d["rest"] * nn(u, arriving)
        )
        dq = d["q_scale"] * (dq - d["qn"] * jnp.sum(d["qn"] * dq, -1, keepdims=True))
        dk = d["k_scale"] * (dk - d["k"] * jnp.sum(d["k"] * dk, -1, keepdims=True))
        for m, part in enumerate((dq, dk, d["beta"] * y)):
            parts[m].append(part)
    for m in range(3):
        grads[m, :count, :] = jnp.concatenate(parts[m], 1) * act[m][1]


def tap_sums(ext, grads, taps):
    count = grads.shape[1] - 8
    for m in range(3):
        dconv = grads[m, :count, :]
        for j in range(KW):
            row = m * KW + j
            taps[row : row + 1, :] = jnp.sum(
                dconv * ext[m, HALO - 3 + j : HALO - 3 + j + count, :], 0, keepdims=True
            )
    taps[3 * KW :, :] = jnp.zeros((16 - 3 * KW, taps.shape[1]), F32)


def raw_part(cw_ref, grads, m, count):
    raw = cw_ref[m, KW - 1 : KW, :] * grads[m, 0:count, :]
    for j in range(KW - 1):
        raw = raw + cw_ref[m, j : j + 1, :] * grads[m, KW - 1 - j : KW - 1 - j + count, :]
    return raw.astype(BF16)


def whole_kernel(
    heads,
    x_hbm,
    w_hbm,
    cw,
    gate,
    beta,
    g,
    out,
    taps_out,
    x,
    w,
    ext,
    grads,
    tail,
    spill,
    pair_out,
    pair_in,
    chain_out,
    chain_in,
    taps,
    rounded,
    total,
    near_out,
    near_in,
    far_out,
    far_in,
    load_sems,
    tail_sems,
    spill_sems,
    pair_send,
    pair_recv,
    chain_send,
    chain_recv,
    taps_send,
    taps_recv,
    near_send,
    near_recv,
    far_send,
    far_recv,
):
    count, depth = x.shape
    ctx, head_axis = lax.axis_size("ctx"), lax.axis_size("head")
    me, head_me = lax.axis_index("ctx"), lax.axis_index("head")
    pairs = ctx // 2
    place, odd = me // 2, me % 2

    def send(src, dst, send_sem, recv_sem, axis, target):
        return pltpu.make_async_remote_copy(
            src_ref=src,
            dst_ref=dst,
            send_sem=send_sem,
            recv_sem=recv_sem,
            device_id={axis: target},
            device_id_type=pl.DeviceIdType.MESH,
        )

    loads = [pltpu.make_async_copy(w_hbm.at[m], w.at[m], load_sems.at[m]) for m in range(3)]
    loads.append(pltpu.make_async_copy(x_hbm, x, load_sems.at[3]))
    for m in (3, 1, 0, 2):
        loads[m].start()
    barrier = pltpu.get_barrier_semaphore()
    for axis, at, size in (("ctx", me, ctx), ("head", head_me, head_axis)):
        for d in range(1, size):
            pl.semaphore_signal(
                barrier,
                inc=1,
                device_id={axis: (at + d) % size},
                device_id_type=pl.DeviceIdType.MESH,
            )
    pl.semaphore_wait(barrier, ctx + head_axis - 2)

    tail_copy = send(
        x_hbm.at[count - HALO :], tail, tail_sems.at[0], tail_sems.at[1], "ctx", (me + 1) % ctx
    )
    tail_copy.start()

    def get_tail():
        tail_copy.wait()
        return jnp.where(me == 0, jnp.zeros_like(tail), tail[...])

    def get_weights(m):
        loads[m].wait()

    loads[3].wait()
    act, per_head = local_part(get_weights, get_tail, x, w, cw, gate, beta, g, ext, heads)
    pair_copies = []
    for h, d in enumerate(per_head):
        for i, name in enumerate("ABC"):
            pair_out[h, i] = d[name].astype(BF16)
        pair_copies.append(
            send(
                pair_out.at[h],
                pair_in.at[h],
                pair_send.at[h],
                pair_recv.at[h],
                "ctx",
                me + 1 - 2 * odd,
            )
        )
        pair_copies[h].start()
    for d in per_head:
        back = tn(d["inv"], jnp.concatenate([d["wg"], d["k_rest"]], 1), True)
        d["y0"], d["kt_rest"] = back[:, :DK], back[:, DK:]
    is_odd = odd == 1
    early, late, merged = [], [], []
    for h, d in enumerate(per_head):
        pair_copies[h].wait()
        own = [d[name] for name in "ABC"]
        other = [pair_in[h, i].astype(F32) for i in range(3)]
        first = [jnp.where(is_odd, o, m) for m, o in zip(own, other)]
        second = [jnp.where(is_odd, m, o) for m, o in zip(own, other)]
        early.append(first)
        late.append(second)
        merged.append(
            (
                nn(first[0], second[0], True),
                nn(first[1], second[0], True) + second[1],
                nt(second[2], first[0], True) + first[2],
            )
        )

    forward_copies, backward_copies = [], []
    for h in range(heads):
        forward_copies.append(
            send(
                chain_out.at[0, h],
                chain_in.at[0, h],
                chain_send.at[0, h],
                chain_recv.at[0, h],
                "ctx",
                (me + 2) % ctx,
            )
        )
        backward_copies.append(
            send(
                chain_out.at[1, h],
                chain_in.at[1, h],
                chain_send.at[1, h],
                chain_recv.at[1, h],
                "ctx",
                (me + ctx - 2) % ctx,
            )
        )

    def forward():
        @pl.when(place == 0)
        def _():
            chain_in[0] = jnp.zeros_like(chain_in[0])

        for h in range(heads):

            @pl.when(place > 0)
            def _():
                forward_copies[h].wait_recv()

            @pl.when(place < pairs - 1)
            def _():
                chain_out[0, h] = (
                    nn(chain_in[0, h], merged[h][0], True) + merged[h][1]
                ).astype(BF16)
                forward_copies[h].start()

    def backward():
        @pl.when(place == pairs - 1)
        def _():
            chain_in[1] = jnp.zeros_like(chain_in[1])

        for h in range(heads):

            @pl.when(place < pairs - 1)
            def _():
                backward_copies[h].wait_recv()

            @pl.when(place > 0)
            def _():
                chain_out[1, h] = (
                    nt(chain_in[1, h], merged[h][0], True) + merged[h][2]
                ).astype(BF16)
                backward_copies[h].start()

    @pl.when(place < pairs // 2)
    def _():
        forward()
        backward()

    @pl.when(place >= pairs // 2)
    def _():
        backward()
        forward()

    states = []
    for h in range(heads):
        start, arriving = chain_in[0, h], chain_in[1, h]
        start_odd = nn(start, early[h][0], True) + early[h][1]
        arriving_even = nt(arriving, late[h][0], True) + late[h][2]
        states.append(
            (
                jnp.where(is_odd, start_odd, start.astype(F32)),
                jnp.where(is_odd, arriving.astype(F32), arriving_even),
            )
        )
    carried_part(act, per_head, cw, ext, grads, states)
    spill_copy = send(
        grads.at[:, 0:8, :], spill, spill_sems.at[0], spill_sems.at[1], "ctx", (me + ctx - 1) % ctx
    )
    spill_copy.start()
    tap_sums(ext, grads, taps.at[me])
    taps_copies = [
        send(
            taps.at[me],
            taps.at[me],
            taps_send.at[d - 1],
            taps_recv.at[d - 1],
            "ctx",
            (me + d) % ctx,
        )
        for d in range(1, ctx)
    ]
    for copy in taps_copies:
        copy.start()
    spill_copy.wait()
    grads[:, count:, :] = jnp.where(me == ctx - 1, jnp.zeros_like(spill), spill[...])
    width = w.shape[2]
    for m in range(3):
        rounded[:, m * width : (m + 1) * width] = raw_part(cw, grads, m, count)
    block = count // head_axis
    chunks, _, span = total.shape
    sibling = head_me + 1 - 2 * (head_me % 2)
    far = (head_me + 2) % 4

    def rows_of(c, owner):
        return total[c, pl.ds(pl.multiple_of(owner * block, 16), block), :]

    near_copies, far_copies = [], []

    def pass_on(c):
        near_copies[c].wait_recv()
        far_out[c] = (rows_of(c, far) + near_in[c, block:].astype(F32)).astype(BF16)
        copy = send(
            far_out.at[c], far_in.at[c], far_send.at[c], far_recv.at[c], "head", far
        )
        copy.start()
        far_copies.append(copy)

    for c in range(chunks):
        part = None
        for m in range(3):
            term = nt(
                rounded[:, m * width : (m + 1) * width], w[m, c * span : (c + 1) * span, :]
            )
            part = term if part is None else part + term
        total[c] = part
        near_out[c, :block] = rows_of(c, sibling).astype(BF16)
        near_out[c, block:] = rows_of(c, (sibling + 2) % 4).astype(BF16)
        copy = send(
            near_out.at[c], near_in.at[c], near_send.at[c], near_recv.at[c], "head", sibling
        )
        copy.start()
        near_copies.append(copy)
        if c > 0:
            pass_on(c - 1)
    pass_on(chunks - 1)
    for copy in taps_copies:
        copy.wait()
    summed = taps[0]
    for i in range(1, ctx):
        summed = summed + taps[i]
    for m in range(3):
        taps_out[m] = summed[m * KW : (m + 1) * KW]
    for c in range(chunks):
        far_copies[c].wait_recv()
        result = rows_of(c, head_me) + near_in[c, :block].astype(F32) + far_in[c].astype(F32)
        out[:, c * span : (c + 1) * span] = result.astype(BF16)
    for copy in near_copies + far_copies:
        copy.wait_send()

    @pl.when(place < pairs - 1)
    def _():
        for copy in forward_copies:
            copy.wait_send()

    @pl.when(place > 0)
    def _():
        for copy in backward_copies:
            copy.wait_send()


def store_kernel(grad, taps, grad_out, taps_out, sems):
    copies = [
        pltpu.make_async_copy(grad, grad_out, sems.at[0]),
        pltpu.make_async_copy(taps, taps_out, sems.at[1]),
    ]
    for copy in copies:
        copy.start()
    for copy in copies:
        copy.wait()


def on_device(inputs, projection, conv_weight, gate_code, beta_code, grad_out):
    count, depth = inputs.shape
    heads = gate_code.shape[0]
    width = heads * DK
    ctx, head_axis = lax.axis_size("ctx"), lax.axis_size("head")
    chunks = 4
    span = depth // chunks
    block = count // head_axis
    dma = pltpu.SemaphoreType.DMA
    input_grad, taps = pl.pallas_call(
        functools.partial(whole_kernel, heads),
        out_shape=(
            jax.ShapeDtypeStruct((block, depth), BF16),
            jax.ShapeDtypeStruct((3, KW, width), F32),
        ),
        in_specs=[ANY, ANY] + [VMEM] * 4,
        out_specs=(VMEM, VMEM),
        scratch_shapes=[
            pltpu.VMEM(inputs.shape, BF16),
            pltpu.VMEM(projection.shape, BF16),
            pltpu.VMEM((3, count + HALO, width), F32),
            pltpu.VMEM((3, count + 8, width), F32),
            pltpu.VMEM((HALO, depth), BF16),
            pltpu.VMEM((3, 8, width), F32),
            pltpu.VMEM((heads, 3, DK, DK), BF16),
            pltpu.VMEM((heads, 3, DK, DK), BF16),
            pltpu.VMEM((2, heads, DK, DK), BF16),
            pltpu.VMEM((2, heads, DK, DK), BF16),
            pltpu.VMEM((ctx, 16, width), F32),
            pltpu.VMEM((count, 3 * width), BF16),
            pltpu.VMEM((chunks, count, span), F32),
            pltpu.VMEM((chunks, 2 * block, span), BF16),
            pltpu.VMEM((chunks, 2 * block, span), BF16),
            pltpu.VMEM((chunks, block, span), BF16),
            pltpu.VMEM((chunks, block, span), BF16),
            dma((4,)),
            dma((2,)),
            dma((2,)),
            dma((heads,)),
            dma((heads,)),
            dma((2, heads)),
            dma((2, heads)),
            dma((ctx - 1,)),
            dma((ctx - 1,)),
            dma((chunks,)),
            dma((chunks,)),
            dma((chunks,)),
            dma((chunks,)),
        ],
        compiler_params=pltpu.CompilerParams(
            collective_id=0, has_side_effects=True, vmem_limit_bytes=56 * 1024 * 1024
        ),
    )(inputs, projection, conv_weight, gate_code, beta_code, grad_out)
    return pl.pallas_call(
        store_kernel,
        out_shape=(
            jax.ShapeDtypeStruct((block, depth), BF16),
            jax.ShapeDtypeStruct((3, KW, width), F32),
        ),
        in_specs=[ANY, ANY],
        out_specs=(ANY, ANY),
        scratch_shapes=[dma((2,))],
    )(input_grad, taps)


def solution(mesh):
    return jax.shard_map(
        on_device,
        mesh=mesh,
        in_specs=(
            P("ctx", None),
            P(None, None, "head"),
            P(None, None, "head"),
            P("head", "ctx"),
            P("head", "ctx"),
            P("ctx", "head"),
        ),
        out_specs=(P(("ctx", "head"), None), P(None, None, "head")),
        check_vma=False,
    )
```

```python
import functools

import jax
import jax.numpy as jnp
from jax import lax
from jax.experimental import pallas as pl
from jax.experimental.pallas import tpu as pltpu
from jax.sharding import PartitionSpec as P

DK = 128
KW = 4
GROUP = 64
HALO = 16
F32 = jnp.float32
BF16 = jnp.bfloat16
VMEM = pl.BlockSpec(memory_space=pltpu.VMEM)
ANY = pl.BlockSpec(memory_space=pl.ANY)


def contract(a, b, dims, precise):
    def one(left, right):
        return lax.dot_general(left, right, (dims, ((), ())), preferred_element_type=F32)

    if not precise:
        return one(a.astype(BF16), b.astype(BF16))
    a_high, b_high = a.astype(BF16), b.astype(BF16)
    total = one(a_high, b_high)
    if b.dtype == F32:
        total = total + one(a_high, (b - b_high.astype(F32)).astype(BF16))
    if a.dtype == F32:
        total = total + one((a - a_high.astype(F32)).astype(BF16), b_high)
    return total


def exact_nt(a, b):
    return lax.dot_general(
        a, b, (((1,), (1,)), ((), ())), precision=lax.Precision.HIGHEST, preferred_element_type=F32
    )


def nn(a, b, precise=False):
    return contract(a, b, ((1,), (0,)), precise)


def nt(a, b, precise=False):
    return contract(a, b, ((1,), (1,)), precise)


def tn(a, b, precise=False):
    return contract(a, b, ((0,), (0,)), precise)


def unit_inverses(lowers, eye, distance):
    count = eye.shape[0]
    inverses = [eye - jnp.where(distance == 1, low, 0.0) for low in lowers]
    size = 2
    while size < count:
        mask = (distance >= size) & (distance < 2 * size)
        inner = [nn(inv, jnp.where(mask, low, 0.0)) for inv, low in zip(inverses, lowers)]
        inverses = [inv - nn(mid, inv) for inv, mid in zip(inverses, inner)]
        size *= 2
    left = [eye - inv - nn(low, inv, True) for inv, low in zip(inverses, lowers)]
    return [inv + nn(inv, rest) for inv, rest in zip(inverses, left)]


def solve_down(d, rows):
    done = []
    for b, inv in enumerate(d["inv"]):
        part = rows[b * GROUP : (b + 1) * GROUP]
        if b > 0:
            part = part - nn(d["off"][b], jnp.concatenate(done, 0), True)
        done.append(nn(inv, part, True))
    return jnp.concatenate(done, 0)


def solve_up(d, rows):
    done = []
    for b in reversed(range(len(d["inv"]))):
        part = tn(d["inv"][b], rows[b * GROUP : (b + 1) * GROUP], True)
        done.insert(0, part)
        if b > 0:
            rows = rows[: b * GROUP] - tn(d["off"][b], part, True)
    return jnp.concatenate(done, 0)


def local_part(get_weights, get_tail, x_ref, w_ref, cw_ref, gate_ref, beta_ref, g_ref, ext, slope, heads):
    count = x_ref.shape[0]
    for m in (1, 0, 2):
        get_weights(m)
        ext[m, HALO:, :] = nn(x_ref[...], w_ref[m]).astype(BF16).astype(F32)
    tail = get_tail()
    for m in range(3):
        ext[m, :HALO, :] = nn(tail, w_ref[m]).astype(BF16).astype(F32)
    rows = lax.broadcasted_iota(jnp.int32, (count, count), 0)
    cols = lax.broadcasted_iota(jnp.int32, (count, count), 1)
    eye = (rows == cols).astype(F32)
    inclusive = (rows >= cols).astype(F32)
    strict = (rows > cols).astype(F32)
    log_gate = jnp.log(1.0 - 0.001 * gate_ref[...].astype(F32) / 1023.0)
    beta_rows = beta_ref[...].astype(F32) / 1023.0
    sums_row = exact_nt(log_gate, inclusive)
    sums_col = exact_nt(inclusive, log_gate)
    beta_cols = exact_nt(eye, beta_rows)
    act = []
    for m in range(3):
        conv = cw_ref[m, 0:1, :] * ext[m, HALO - 3 : HALO - 3 + count, :]
        for j in range(1, KW):
            conv = conv + cw_ref[m, j : j + 1, :] * ext[m, HALO - 3 + j : HALO - 3 + j + count, :]
        sig = jax.nn.sigmoid(conv)
        act.append(conv * sig)
        slope[m] = conv
    out = []
    for h in range(heads):
        lanes = slice(h * DK, (h + 1) * DK)
        q_act, k_act, v = (act[m][:, lanes] for m in range(3))
        q_scale = lax.rsqrt(jnp.sum(q_act * q_act, -1, keepdims=True) + 1e-6)
        k_scale = lax.rsqrt(jnp.sum(k_act * k_act, -1, keepdims=True) + 1e-6)
        qn = q_act * q_scale
        s_col = sums_col[:, h : h + 1]
        beta = beta_cols[:, h : h + 1]
        total = s_col[count - 1 : count, :]
        d = dict(
            q=qn * DK**-0.5,
            k=k_act * k_scale,
            v=v,
            q_scale=q_scale * DK**-0.5,
            k_scale=k_scale,
            qn=qn,
            beta=beta,
            now=jnp.exp(s_col),
            rest=jnp.exp(total - s_col),
            whole=jnp.exp(total),
            g=g_ref[:, lanes],
        )
        d["s_col"], d["s_row"] = s_col, sums_row[h : h + 1, :]
        d["beta_row"] = beta_rows[h : h + 1, :]
        d["low"], d["off"] = [], []
        for b in range(count // GROUP):
            here, before = slice(b * GROUP, (b + 1) * GROUP), slice(0, b * GROUP)
            keys = d["k"][here]
            scale = jnp.exp(s_col[here] - d["s_row"][:, here]) * strict[:GROUP, :GROUP]
            d["low"].append(nt(keys, keys, True) * (scale * beta[here]))
            if b > 0:
                scale = jnp.exp(s_col[here] - d["s_row"][:, before]) * beta[here]
                d["off"].append(nt(keys, d["k"][before], True) * scale)
            else:
                d["off"].append(None)
        out.append(d)
    blocks = count // GROUP
    inverses = unit_inverses(
        [low for d in out for low in d["low"]],
        eye[:GROUP, :GROUP],
        rows[:GROUP, :GROUP] ^ cols[:GROUP, :GROUP],
    )
    for h, d in enumerate(out):
        d["inv"] = inverses[h * blocks : (h + 1) * blocks]
        d["k_rest"] = d["rest"] * d["k"]
        d["k_now"] = (d["beta"] * d["now"]) * d["k"]
        solved = solve_down(d, jnp.concatenate([d["beta"] * d["v"], d["k_now"]], 1))
        d["u0"] = solved[:, :DK]
        d["kt"] = solved[:, DK:]
        both = tn(solved, d["k_rest"], True)
        d["B"] = both[:DK]
        d["A"] = d["whole"] * eye[:DK, :DK] - both[DK:]
    return out


def adjoint_part(per_head):
    for d in per_head:
        count = d["k"].shape[0]
        rows = lax.broadcasted_iota(jnp.int32, (count, count), 0)
        cols = lax.broadcasted_iota(jnp.int32, (count, count), 1)
        decay = jnp.exp(d["s_col"] - d["s_row"])
        d["between"] = jnp.where(rows >= cols, decay, 0.0)
        d["scores"] = nt(d["q"], d["k"], True) * d["between"]
        d["wg"] = tn(d["scores"], d["g"], True)
        d["C"] = tn(d["g"], d["now"] * d["q"], True) - tn(d["wg"], d["kt"], True)


def prepared_part(per_head, slope):
    for m in range(3):
        sig = jax.nn.sigmoid(slope[m])
        slope[m] = sig * (1.0 + slope[m] * (1.0 - sig))
    for d in per_head:
        count = d["k"].shape[0]
        back = solve_up(d, jnp.concatenate([d["wg"], d["k_rest"]], 1))
        d["y0"], d["kt_rest"] = back[:, :DK], back[:, DK:]
        rows = lax.broadcasted_iota(jnp.int32, (count, count), 0)
        cols = lax.broadcasted_iota(jnp.int32, (count, count), 1)
        d["low_scale"] = jnp.where(rows > cols, -d["beta"] * d["between"], 0.0)
        turned = jnp.exp(d["s_row"] - d["s_col"])
        d["between_t"] = jnp.where(rows <= cols, turned, 0.0)
        d["low_scale_t"] = jnp.where(rows < cols, -d["beta_row"] * turned, 0.0)


def carried_part(per_head, slope, grads, states):
    count = grads.shape[1] - 8
    parts = [[], [], []]
    for d, (start, arriving) in zip(per_head, states):
        u = d["u0"] - nt(d["kt"], start, True)
        y = d["y0"] + nt(d["kt_rest"], arriving, True)
        keys, asks = d["k"].astype(BF16), d["q"].astype(BF16)
        u_low, y_low = u.astype(BF16), y.astype(BF16)
        start_low, arriving_low = start.astype(BF16), arriving.astype(BF16)
        low = d["low_scale"] * nt(y_low, u_low)
        low_t = d["low_scale_t"] * nt(u_low, y_low)
        seen = d["between"] * nt(d["g"], u_low)
        seen_t = d["between_t"] * nt(u_low, d["g"])
        dq = d["now"] * nn(d["g"], start_low) + nn(seen, keys)
        dk = (
            nn(low, keys)
            + nn(low_t, keys)
            + nn(seen_t, asks)
            - (d["beta"] * d["now"]) * nn(y_low, start_low)
            + d["rest"] * nn(u_low, arriving_low)
        )
        dq = d["q_scale"] * (dq - d["qn"] * jnp.sum(d["qn"] * dq, -1, keepdims=True))
        dk = d["k_scale"] * (dk - d["k"] * jnp.sum(d["k"] * dk, -1, keepdims=True))
        for m, part in enumerate((dq, dk, d["beta"] * y)):
            parts[m].append(part)
    for m in range(3):
        grads[m, :count, :] = jnp.concatenate(parts[m], 1) * slope[m]


def tap_sums(ext, grads, taps):
    count = grads.shape[1] - 8
    for m in range(3):
        dconv = grads[m, :count, :]
        for j in range(KW):
            row = m * KW + j
            taps[row : row + 1, :] = jnp.sum(
                dconv * ext[m, HALO - 3 + j : HALO - 3 + j + count, :], 0, keepdims=True
            )
    taps[3 * KW :, :] = jnp.zeros((16 - 3 * KW, taps.shape[1]), F32)


def raw_part(cw_ref, grads, m, at, count):
    raw = cw_ref[m, KW - 1 : KW, :] * grads[m, at : at + count, :]
    for j in range(KW - 1):
        first = at + KW - 1 - j
        raw = raw + cw_ref[m, j : j + 1, :] * grads[m, first : first + count, :]
    return raw.astype(BF16)


def whole_kernel(
    heads,
    x_hbm,
    w_hbm,
    cw,
    gate,
    beta,
    g,
    out,
    taps_out,
    x,
    w,
    ext,
    slope,
    grads,
    tail,
    spill,
    pair_out,
    pair_in,
    chain_out,
    chain_in,
    taps,
    rounded,
    total,
    near_out,
    near_in,
    far_out,
    far_in,
    load_sems,
    tail_sems,
    spill_sems,
    pair_send,
    pair_recv,
    chain_send,
    chain_recv,
    taps_send,
    taps_recv,
    near_send,
    near_recv,
    far_send,
    far_recv,
):
    count, depth = x.shape
    ctx, head_axis = lax.axis_size("ctx"), lax.axis_size("head")
    me, head_me = lax.axis_index("ctx"), lax.axis_index("head")
    pairs = ctx // 2
    place, odd = me // 2, me % 2

    def send(src, dst, send_sem, recv_sem, axis, target):
        return pltpu.make_async_remote_copy(
            src_ref=src,
            dst_ref=dst,
            send_sem=send_sem,
            recv_sem=recv_sem,
            device_id={axis: target},
            device_id_type=pl.DeviceIdType.MESH,
        )

    loads = [pltpu.make_async_copy(w_hbm.at[m], w.at[m], load_sems.at[m]) for m in range(3)]
    loads.append(pltpu.make_async_copy(x_hbm, x, load_sems.at[3]))
    for m in (3, 1, 0, 2):
        loads[m].start()
    barrier = pltpu.get_barrier_semaphore()
    for axis, at, size in (("ctx", me, ctx), ("head", head_me, head_axis)):
        for d in range(1, size):
            pl.semaphore_signal(
                barrier,
                inc=1,
                device_id={axis: (at + d) % size},
                device_id_type=pl.DeviceIdType.MESH,
            )
    pl.semaphore_wait(barrier, ctx + head_axis - 2)

    tail_copy = send(
        x_hbm.at[count - HALO :], tail, tail_sems.at[0], tail_sems.at[1], "ctx", (me + 1) % ctx
    )
    tail_copy.start()

    def get_tail():
        tail_copy.wait()
        return jnp.where(me == 0, jnp.zeros_like(tail), tail[...])

    def get_weights(m):
        loads[m].wait()

    loads[3].wait()
    per_head = local_part(get_weights, get_tail, x, w, cw, gate, beta, g, ext, slope, heads)
    pair_copies = []

    def send_pair(h, first, names):
        for i, name in enumerate(names):
            pair_out[h, first + i] = per_head[h][name].astype(BF16)
        part = pl.ds(first, len(names))
        copy = send(
            pair_out.at[h, part],
            pair_in.at[h, part],
            pair_send.at[h, first // 2],
            pair_recv.at[h, first // 2],
            "ctx",
            me + 1 - 2 * odd,
        )
        copy.start()
        pair_copies.append(copy)

    for h in range(heads):
        send_pair(h, 0, "AB")
    adjoint_part(per_head)
    for h in range(heads):
        send_pair(h, 2, "C")
    prepared_part(per_head, slope)
    is_odd = odd == 1
    early, late, merged = [], [], []
    for h, d in enumerate(per_head):
        pair_copies[h].wait()
        pair_copies[heads + h].wait()
        own = [d[name] for name in "ABC"]
        other = [pair_in[h, i].astype(F32) for i in range(3)]
        first = [jnp.where(is_odd, o, m) for m, o in zip(own, other)]
        second = [jnp.where(is_odd, m, o) for m, o in zip(own, other)]
        early.append(first)
        late.append(second)
        merged.append(
            (
                nn(first[0], second[0], True),
                nn(first[1], second[0], True) + second[1],
                nt(second[2], first[0], True) + first[2],
            )
        )

    forward_copies, backward_copies = [], []
    for h in range(heads):
        forward_copies.append(
            send(
                chain_out.at[0, h],
                chain_in.at[0, h],
                chain_send.at[0, h],
                chain_recv.at[0, h],
                "ctx",
                (me + 2) % ctx,
            )
        )
        backward_copies.append(
            send(
                chain_out.at[1, h],
                chain_in.at[1, h],
                chain_send.at[1, h],
                chain_recv.at[1, h],
                "ctx",
                (me + ctx - 2) % ctx,
            )
        )

    def forward():
        @pl.when(place == 0)
        def _():
            chain_in[0] = jnp.zeros_like(chain_in[0])

        for h in range(heads):

            @pl.when(place > 0)
            def _():
                forward_copies[h].wait_recv()

            @pl.when(place < pairs - 1)
            def _():
                chain_out[0, h] = (
                    nn(chain_in[0, h], merged[h][0], True) + merged[h][1]
                ).astype(BF16)
                forward_copies[h].start()

    def backward():
        @pl.when(place == pairs - 1)
        def _():
            chain_in[1] = jnp.zeros_like(chain_in[1])

        for h in range(heads):

            @pl.when(place < pairs - 1)
            def _():
                backward_copies[h].wait_recv()

            @pl.when(place > 0)
            def _():
                chain_out[1, h] = (
                    nt(chain_in[1, h], merged[h][0], True) + merged[h][2]
                ).astype(BF16)
                backward_copies[h].start()

    @pl.when(place < pairs // 2)
    def _():
        forward()
        backward()

    @pl.when(place >= pairs // 2)
    def _():
        backward()
        forward()

    states = []
    for h in range(heads):
        start, arriving = chain_in[0, h], chain_in[1, h]
        start_odd = nn(start, early[h][0], True) + early[h][1]
        arriving_even = nt(arriving, late[h][0], True) + late[h][2]
        states.append(
            (
                jnp.where(is_odd, start_odd, start.astype(F32)),
                jnp.where(is_odd, arriving.astype(F32), arriving_even),
            )
        )
    carried_part(per_head, slope, grads, states)
    spill_copy = send(
        grads.at[:, 0:8, :], spill, spill_sems.at[0], spill_sems.at[1], "ctx", (me + ctx - 1) % ctx
    )
    spill_copy.start()
    tap_sums(ext, grads, taps.at[me])
    taps_copies = [
        send(
            taps.at[me],
            taps.at[me],
            taps_send.at[d - 1],
            taps_recv.at[d - 1],
            "ctx",
            (me + d) % ctx,
        )
        for d in range(1, ctx)
    ]
    for copy in taps_copies:
        copy.start()
    width = w.shape[2]
    edge = count - 16
    chunks, _, span = total.shape

    def product(c, rows):
        part = None
        for m in range(3):
            term = nt(
                rounded[rows, m * width : (m + 1) * width], w[m, c * span : (c + 1) * span, :]
            )
            part = term if part is None else part + term
        total[c, rows] = part

    for m in range(3):
        rounded[:edge, m * width : (m + 1) * width] = raw_part(cw, grads, m, 0, edge)
    product(0, slice(0, edge))
    spill_copy.wait()
    grads[:, count:, :] = jnp.where(me == ctx - 1, jnp.zeros_like(spill), spill[...])
    for m in range(3):
        rounded[edge:, m * width : (m + 1) * width] = raw_part(cw, grads, m, edge, 16)
    product(0, slice(edge, count))
    block = count // head_axis
    sibling = head_me + 1 - 2 * (head_me % 2)
    far = (head_me + 2) % 4

    def rows_of(c, owner):
        return total[c, pl.ds(pl.multiple_of(owner * block, 16), block), :]

    near_copies, far_copies = [], []

    def pass_on(c):
        near_copies[c].wait_recv()
        far_out[c] = (rows_of(c, far) + near_in[c, block:].astype(F32)).astype(BF16)
        copy = send(
            far_out.at[c], far_in.at[c], far_send.at[c], far_recv.at[c], "head", far
        )
        copy.start()
        far_copies.append(copy)

    for c in range(chunks):
        if c > 0:
            product(c, slice(0, count))
        near_out[c, :block] = rows_of(c, sibling).astype(BF16)
        near_out[c, block:] = rows_of(c, (sibling + 2) % 4).astype(BF16)
        copy = send(
            near_out.at[c], near_in.at[c], near_send.at[c], near_recv.at[c], "head", sibling
        )
        copy.start()
        near_copies.append(copy)
        if c > 0:
            pass_on(c - 1)
    pass_on(chunks - 1)
    for copy in taps_copies:
        copy.wait()
    summed = taps[0]
    for i in range(1, ctx):
        summed = summed + taps[i]
    for m in range(3):
        taps_out[m] = summed[m * KW : (m + 1) * KW]
    for c in range(chunks):
        far_copies[c].wait_recv()
        result = rows_of(c, head_me) + near_in[c, :block].astype(F32) + far_in[c].astype(F32)
        out[:, c * span : (c + 1) * span] = result.astype(BF16)
    for copy in near_copies + far_copies:
        copy.wait_send()

    @pl.when(place < pairs - 1)
    def _():
        for copy in forward_copies:
            copy.wait_send()

    @pl.when(place > 0)
    def _():
        for copy in backward_copies:
            copy.wait_send()


def store_kernel(grad, taps, grad_out, taps_out):
    grad_out[...] = grad[...]
    taps_out[...] = taps[...]


def on_device(inputs, projection, conv_weight, gate_code, beta_code, grad_out):
    count, depth = inputs.shape
    heads = gate_code.shape[0]
    width = heads * DK
    ctx, head_axis = lax.axis_size("ctx"), lax.axis_size("head")
    chunks = 4
    span = depth // chunks
    block = count // head_axis
    dma = pltpu.SemaphoreType.DMA
    input_grad, taps = pl.pallas_call(
        functools.partial(whole_kernel, heads),
        out_shape=(
            jax.ShapeDtypeStruct((block, depth), BF16),
            jax.ShapeDtypeStruct((3, KW, width), F32),
        ),
        in_specs=[ANY, ANY] + [VMEM] * 4,
        out_specs=(VMEM, VMEM),
        scratch_shapes=[
            pltpu.VMEM(inputs.shape, BF16),
            pltpu.VMEM(projection.shape, BF16),
            pltpu.VMEM((3, count + HALO, width), F32),
            pltpu.VMEM((3, count, width), F32),
            pltpu.VMEM((3, count + 8, width), F32),
            pltpu.VMEM((HALO, depth), BF16),
            pltpu.VMEM((3, 8, width), F32),
            pltpu.VMEM((heads, 3, DK, DK), BF16),
            pltpu.VMEM((heads, 3, DK, DK), BF16),
            pltpu.VMEM((2, heads, DK, DK), BF16),
            pltpu.VMEM((2, heads, DK, DK), BF16),
            pltpu.VMEM((ctx, 16, width), F32),
            pltpu.VMEM((count, 3 * width), BF16),
            pltpu.VMEM((chunks, count, span), F32),
            pltpu.VMEM((chunks, 2 * block, span), BF16),
            pltpu.VMEM((chunks, 2 * block, span), BF16),
            pltpu.VMEM((chunks, block, span), BF16),
            pltpu.VMEM((chunks, block, span), BF16),
            dma((4,)),
            dma((2,)),
            dma((2,)),
            dma((heads, 2)),
            dma((heads, 2)),
            dma((2, heads)),
            dma((2, heads)),
            dma((ctx - 1,)),
            dma((ctx - 1,)),
            dma((chunks,)),
            dma((chunks,)),
            dma((chunks,)),
            dma((chunks,)),
        ],
        compiler_params=pltpu.CompilerParams(
            collective_id=0, has_side_effects=True, vmem_limit_bytes=56 * 1024 * 1024
        ),
    )(inputs, projection, conv_weight, gate_code, beta_code, grad_out)
    return pl.pallas_call(
        store_kernel,
        out_shape=(
            jax.ShapeDtypeStruct((block, depth), BF16),
            jax.ShapeDtypeStruct((3, KW, width), F32),
        ),
        in_specs=[VMEM, VMEM],
        out_specs=(VMEM, VMEM),
    )(input_grad, taps)


def solution(mesh):
    return jax.shard_map(
        on_device,
        mesh=mesh,
        in_specs=(
            P("ctx", None),
            P(None, None, "head"),
            P(None, None, "head"),
            P("head", "ctx"),
            P("head", "ctx"),
            P("ctx", "head"),
        ),
        out_specs=(P(("ctx", "head"), None), P(None, None, "head")),
        check_vma=False,
    )
```

```python
import functools

import jax
import jax.numpy as jnp
from jax import lax
from jax.experimental import pallas as pl
from jax.experimental.pallas import tpu as pltpu
from jax.sharding import PartitionSpec as P

DK = 128
KW = 4
GROUP = 64
HALO = 16
F32 = jnp.float32
BF16 = jnp.bfloat16
VMEM = pl.BlockSpec(memory_space=pltpu.VMEM)
ANY = pl.BlockSpec(memory_space=pl.ANY)


def contract(a, b, dims, precise):
    def one(left, right):
        return lax.dot_general(left, right, (dims, ((), ())), preferred_element_type=F32)

    if not precise:
        return one(a.astype(BF16), b.astype(BF16))
    a_high, b_high = a.astype(BF16), b.astype(BF16)
    total = one(a_high, b_high)
    if b.dtype == F32:
        total = total + one(a_high, (b - b_high.astype(F32)).astype(BF16))
    if a.dtype == F32:
        total = total + one((a - a_high.astype(F32)).astype(BF16), b_high)
    return total


def exact_nt(a, b):
    return lax.dot_general(
        a, b, (((1,), (1,)), ((), ())), precision=lax.Precision.HIGHEST, preferred_element_type=F32
    )


def nn(a, b, precise=False):
    return contract(a, b, ((1,), (0,)), precise)


def nt(a, b, precise=False):
    return contract(a, b, ((1,), (1,)), precise)


def tn(a, b, precise=False):
    return contract(a, b, ((0,), (0,)), precise)


def unit_inverses(lowers, eye, distance):
    count = eye.shape[0]
    inverses = [eye - jnp.where(distance == 1, low, 0.0) for low in lowers]
    size = 2
    while size < count:
        mask = (distance >= size) & (distance < 2 * size)
        inner = [nn(inv, jnp.where(mask, low, 0.0)) for inv, low in zip(inverses, lowers)]
        inverses = [inv - nn(mid, inv) for inv, mid in zip(inverses, inner)]
        size *= 2
    left = [eye - inv - nn(low, inv, True) for inv, low in zip(inverses, lowers)]
    return [inv + nn(inv, rest) for inv, rest in zip(inverses, left)]


def solve_down(d, rows):
    done = []
    for b, inv in enumerate(d["inv"]):
        part = rows[b * GROUP : (b + 1) * GROUP]
        if b > 0:
            part = part - nn(d["off"][b], jnp.concatenate(done, 0), True)
        done.append(nn(inv, part, True))
    return jnp.concatenate(done, 0)


def solve_up(d, rows):
    done = []
    for b in reversed(range(len(d["inv"]))):
        part = tn(d["inv"][b], rows[b * GROUP : (b + 1) * GROUP], True)
        done.insert(0, part)
        if b > 0:
            rows = rows[: b * GROUP] - tn(d["off"][b], part, True)
    return jnp.concatenate(done, 0)


def local_part(get_weights, get_tail, x_ref, w_ref, cw_ref, gate_ref, beta_ref, g_ref, ext, slope, heads):
    count = x_ref.shape[0]
    for m in (1, 0, 2):
        get_weights(m)
        ext[m, HALO:, :] = nn(x_ref[...], w_ref[m]).astype(BF16).astype(F32)
    for n in range(4, 8):
        get_weights(n)
    tail = get_tail()
    for m in range(3):
        ext[m, :HALO, :] = nn(tail, w_ref[m]).astype(BF16).astype(F32)
    rows = lax.broadcasted_iota(jnp.int32, (count, count), 0)
    cols = lax.broadcasted_iota(jnp.int32, (count, count), 1)
    eye = (rows == cols).astype(F32)
    inclusive = (rows >= cols).astype(F32)
    strict = (rows > cols).astype(F32)
    log_gate = jnp.log(1.0 - 0.001 * gate_ref[...].astype(F32) / 1023.0)
    beta_rows = beta_ref[...].astype(F32) / 1023.0
    sums_row = exact_nt(log_gate, inclusive)
    sums_col = exact_nt(inclusive, log_gate)
    beta_cols = exact_nt(eye, beta_rows)
    act = []
    for m in range(3):
        conv = cw_ref[m, 0:1, :] * ext[m, HALO - 3 : HALO - 3 + count, :]
        for j in range(1, KW):
            conv = conv + cw_ref[m, j : j + 1, :] * ext[m, HALO - 3 + j : HALO - 3 + j + count, :]
        sig = jax.nn.sigmoid(conv)
        act.append(conv * sig)
        slope[m] = conv
    out = []
    for h in range(heads):
        lanes = slice(h * DK, (h + 1) * DK)
        q_act, k_act, v = (act[m][:, lanes] for m in range(3))
        q_scale = lax.rsqrt(jnp.sum(q_act * q_act, -1, keepdims=True) + 1e-6)
        k_scale = lax.rsqrt(jnp.sum(k_act * k_act, -1, keepdims=True) + 1e-6)
        qn = q_act * q_scale
        s_col = sums_col[:, h : h + 1]
        beta = beta_cols[:, h : h + 1]
        total = s_col[count - 1 : count, :]
        d = dict(
            q=qn * DK**-0.5,
            k=k_act * k_scale,
            v=v,
            q_scale=q_scale * DK**-0.5,
            k_scale=k_scale,
            qn=qn,
            beta=beta,
            now=jnp.exp(s_col),
            rest=jnp.exp(total - s_col),
            whole=jnp.exp(total),
            g=g_ref[:, lanes],
        )
        d["s_col"], d["s_row"] = s_col, sums_row[h : h + 1, :]
        d["beta_row"] = beta_rows[h : h + 1, :]
        d["low"], d["off"] = [], []
        for b in range(count // GROUP):
            here, before = slice(b * GROUP, (b + 1) * GROUP), slice(0, b * GROUP)
            keys = d["k"][here]
            scale = jnp.exp(s_col[here] - d["s_row"][:, here]) * strict[:GROUP, :GROUP]
            d["low"].append(nt(keys, keys, True) * (scale * beta[here]))
            if b > 0:
                scale = jnp.exp(s_col[here] - d["s_row"][:, before]) * beta[here]
                d["off"].append(nt(keys, d["k"][before], True) * scale)
            else:
                d["off"].append(None)
        out.append(d)
    for d in out:
        d["between"] = jnp.exp(d["s_col"] - d["s_row"]) * inclusive
        d["scores"] = nt(d["q"], d["k"], True) * d["between"]
        d["wg"] = tn(d["scores"], d["g"], True)
    blocks = count // GROUP
    inverses = unit_inverses(
        [low for d in out for low in d["low"]],
        eye[:GROUP, :GROUP],
        rows[:GROUP, :GROUP] ^ cols[:GROUP, :GROUP],
    )
    for h, d in enumerate(out):
        d["inv"] = inverses[h * blocks : (h + 1) * blocks]
        d["k_rest"] = d["rest"] * d["k"]
        d["k_now"] = (d["beta"] * d["now"]) * d["k"]
        solved = solve_down(d, jnp.concatenate([d["beta"] * d["v"], d["k_now"]], 1))
        d["u0"] = solved[:, :DK]
        d["kt"] = solved[:, DK:]
        both = tn(solved, d["k_rest"], True)
        d["B"] = both[:DK]
        d["A"] = d["whole"] * eye[:DK, :DK] - both[DK:]
        d["C"] = tn(d["g"], d["now"] * d["q"], True) - tn(d["wg"], d["kt"], True)
    return out


def prepared_part(per_head, slope):
    for m in range(3):
        sig = jax.nn.sigmoid(slope[m])
        slope[m] = sig * (1.0 + slope[m] * (1.0 - sig))
    for d in per_head:
        count = d["k"].shape[0]
        back = solve_up(d, jnp.concatenate([d["wg"], d["k_rest"]], 1))
        d["y0"], d["kt_rest"] = back[:, :DK], back[:, DK:]
        rows = lax.broadcasted_iota(jnp.int32, (count, count), 0)
        cols = lax.broadcasted_iota(jnp.int32, (count, count), 1)
        d["low_scale"] = jnp.where(rows > cols, -d["beta"] * d["between"], 0.0)
        turned = jnp.exp(d["s_row"] - d["s_col"])
        d["between_t"] = jnp.where(rows <= cols, turned, 0.0)
        d["low_scale_t"] = jnp.where(rows < cols, -d["beta_row"] * turned, 0.0)


def carried_part(per_head, slope, grads, states):
    count = grads.shape[1] - 8
    parts = [[], [], []]
    for d, (start, arriving) in zip(per_head, states):
        u = d["u0"] - nt(d["kt"], start, True)
        y = d["y0"] + nt(d["kt_rest"], arriving, True)
        keys, asks = d["k"].astype(BF16), d["q"].astype(BF16)
        u_low, y_low = u.astype(BF16), y.astype(BF16)
        start_low, arriving_low = start.astype(BF16), arriving.astype(BF16)
        low = d["low_scale"] * nt(y_low, u_low)
        low_t = d["low_scale_t"] * nt(u_low, y_low)
        seen = d["between"] * nt(d["g"], u_low)
        seen_t = d["between_t"] * nt(u_low, d["g"])
        dq = d["now"] * nn(d["g"], start_low) + nn(seen, keys)
        dk = (
            nn(low, keys)
            + nn(low_t, keys)
            + nn(seen_t, asks)
            - (d["beta"] * d["now"]) * nn(y_low, start_low)
            + d["rest"] * nn(u_low, arriving_low)
        )
        dq = d["q_scale"] * (dq - d["qn"] * jnp.sum(d["qn"] * dq, -1, keepdims=True))
        dk = d["k_scale"] * (dk - d["k"] * jnp.sum(d["k"] * dk, -1, keepdims=True))
        for m, part in enumerate((dq, dk, d["beta"] * y)):
            parts[m].append(part)
    for m in range(3):
        grads[m, :count, :] = jnp.concatenate(parts[m], 1) * slope[m]


def tap_sums(ext, grads, taps):
    count = grads.shape[1] - 8
    for m in range(3):
        dconv = grads[m, :count, :]
        for j in range(KW):
            row = m * KW + j
            taps[row : row + 1, :] = jnp.sum(
                dconv * ext[m, HALO - 3 + j : HALO - 3 + j + count, :], 0, keepdims=True
            )
    taps[3 * KW :, :] = jnp.zeros((16 - 3 * KW, taps.shape[1]), F32)


def raw_part(cw_ref, grads, m, at, count):
    raw = cw_ref[m, KW - 1 : KW, :] * grads[m, at : at + count, :]
    for j in range(KW - 1):
        first = at + KW - 1 - j
        raw = raw + cw_ref[m, j : j + 1, :] * grads[m, first : first + count, :]
    return raw.astype(BF16)


def whole_kernel(
    heads,
    x_hbm,
    w_hbm,
    cw_hbm,
    gate_hbm,
    beta_hbm,
    g_hbm,
    out,
    taps_out,
    x,
    w,
    cw,
    gate,
    beta,
    g,
    merged,
    ext,
    slope,
    grads,
    tail,
    spill,
    pair_out,
    pair_in,
    chain_out,
    chain_in,
    taps,
    rounded,
    total,
    near_out,
    near_in,
    far_out,
    far_in,
    load_sems,
    tail_sems,
    spill_sems,
    pair_send,
    pair_recv,
    chain_send,
    chain_recv,
    taps_send,
    taps_recv,
    near_send,
    near_recv,
    far_send,
    far_recv,
):
    count, depth = x.shape
    ctx, head_axis = lax.axis_size("ctx"), lax.axis_size("head")
    me, head_me = lax.axis_index("ctx"), lax.axis_index("head")
    pairs = ctx // 2
    place, odd = me // 2, me % 2

    def send(src, dst, send_sem, recv_sem, axis, target):
        return pltpu.make_async_remote_copy(
            src_ref=src,
            dst_ref=dst,
            send_sem=send_sem,
            recv_sem=recv_sem,
            device_id={axis: target},
            device_id_type=pl.DeviceIdType.MESH,
        )

    loads = [pltpu.make_async_copy(w_hbm.at[m], w.at[m], load_sems.at[m]) for m in range(3)]
    others = ((x_hbm, x), (cw_hbm, cw), (gate_hbm, gate), (beta_hbm, beta), (g_hbm, g))
    for n, (src, dst) in enumerate(others):
        loads.append(pltpu.make_async_copy(src, dst, load_sems.at[3 + n]))
    barrier = pltpu.get_barrier_semaphore()
    for axis, at, size in (("ctx", me, ctx), ("head", head_me, head_axis)):
        for d in range(1, size):
            pl.semaphore_signal(
                barrier,
                inc=1,
                device_id={axis: (at + d) % size},
                device_id_type=pl.DeviceIdType.MESH,
            )
    for m in (3, 1, 0, 2, 4, 5, 6, 7):
        loads[m].start()
    pl.semaphore_wait(barrier, ctx + head_axis - 2)

    tail_copy = send(
        x_hbm.at[count - HALO :], tail, tail_sems.at[0], tail_sems.at[1], "ctx", (me + 1) % ctx
    )
    tail_copy.start()

    def get_tail():
        tail_copy.wait()
        return jnp.where(me == 0, jnp.zeros_like(tail), tail[...])

    def get_weights(m):
        loads[m].wait()

    loads[3].wait()
    per_head = local_part(get_weights, get_tail, x, w, cw, gate, beta, g, ext, slope, heads)
    pair_copies = []

    half = place < pairs // 2
    for h, d in enumerate(per_head):
        pair_out[h, 0] = d["A"].astype(BF16)
        pair_out[h, 1] = jnp.where(half, d["B"], d["C"]).astype(BF16)
        pair_out[h, 2] = jnp.where(half, d["C"], d["B"]).astype(BF16)
    for n, part in enumerate((pl.ds(0, 2), pl.ds(2, 1))):
        for h in range(heads):
            copy = send(
                pair_out.at[h, part],
                pair_in.at[h, part],
                pair_send.at[h, n],
                pair_recv.at[h, n],
                "ctx",
                me + 1 - 2 * odd,
            )
            copy.start()
            pair_copies.append(copy)
    prepared_part(per_head, slope)
    is_odd = odd == 1

    def ordered(h, name, slot):
        own, other = per_head[h][name], pair_in[h, slot].astype(F32)
        return jnp.where(is_odd, other, own), jnp.where(is_odd, own, other)

    def merge_forward(slot):
        for h in range(heads):
            (_, a_late), (b_early, b_late) = ordered(h, "A", 0), ordered(h, "B", slot)
            merged[h, 1] = nn(b_early, a_late, True) + b_late

    def merge_backward(slot):
        for h in range(heads):
            (a_early, _), (c_early, c_late) = ordered(h, "A", 0), ordered(h, "C", slot)
            merged[h, 2] = nt(c_late, a_early, True) + c_early

    def wait_rest():
        for copy in pair_copies[heads:]:
            copy.wait_recv()

    for h in range(heads):
        pair_copies[h].wait_recv()
        a_early, a_late = ordered(h, "A", 0)
        merged[h, 0] = nn(a_early, a_late, True)

    forward_copies, backward_copies = [], []
    for h in range(heads):
        forward_copies.append(
            send(
                chain_out.at[0, h],
                chain_in.at[0, h],
                chain_send.at[0, h],
                chain_recv.at[0, h],
                "ctx",
                (me + 2) % ctx,
            )
        )
        backward_copies.append(
            send(
                chain_out.at[1, h],
                chain_in.at[1, h],
                chain_send.at[1, h],
                chain_recv.at[1, h],
                "ctx",
                (me + ctx - 2) % ctx,
            )
        )

    def forward():
        @pl.when(place == 0)
        def _():
            chain_in[0] = jnp.zeros_like(chain_in[0])

        for h in range(heads):

            @pl.when(place > 0)
            def _():
                forward_copies[h].wait_recv()

            @pl.when(place < pairs - 1)
            def _():
                chain_out[0, h] = (
                    nn(chain_in[0, h], merged[h, 0], True) + merged[h, 1]
                ).astype(BF16)
                forward_copies[h].start()

    def backward():
        @pl.when(place == pairs - 1)
        def _():
            chain_in[1] = jnp.zeros_like(chain_in[1])

        for h in range(heads):

            @pl.when(place < pairs - 1)
            def _():
                backward_copies[h].wait_recv()

            @pl.when(place > 0)
            def _():
                chain_out[1, h] = (
                    nt(chain_in[1, h], merged[h, 0], True) + merged[h, 2]
                ).astype(BF16)
                backward_copies[h].start()

    @pl.when(half)
    def _():
        merge_forward(1)
        forward()
        wait_rest()
        merge_backward(2)
        backward()

    @pl.when(place >= pairs // 2)
    def _():
        merge_backward(1)
        backward()
        wait_rest()
        merge_forward(2)
        forward()

    states = []
    for h in range(heads):
        start, arriving = chain_in[0, h], chain_in[1, h]
        a_early, a_late = ordered(h, "A", 0)
        other_b = jnp.where(half, pair_in[h, 1], pair_in[h, 2]).astype(F32)
        other_c = jnp.where(half, pair_in[h, 2], pair_in[h, 1]).astype(F32)
        b_early = jnp.where(is_odd, other_b, per_head[h]["B"])
        c_late = jnp.where(is_odd, per_head[h]["C"], other_c)
        start_odd = nn(start, a_early, True) + b_early
        arriving_even = nt(arriving, a_late, True) + c_late
        states.append(
            (
                jnp.where(is_odd, start_odd, start.astype(F32)),
                jnp.where(is_odd, arriving.astype(F32), arriving_even),
            )
        )
    carried_part(per_head, slope, grads, states)
    spill_copy = send(
        grads.at[:, 0:8, :], spill, spill_sems.at[0], spill_sems.at[1], "ctx", (me + ctx - 1) % ctx
    )
    spill_copy.start()
    tap_sums(ext, grads, taps.at[me])
    taps_copies = [
        send(
            taps.at[me],
            taps.at[me],
            taps_send.at[d - 1],
            taps_recv.at[d - 1],
            "ctx",
            (me + d) % ctx,
        )
        for d in range(1, ctx)
    ]
    for copy in taps_copies:
        copy.start()
    width = w.shape[2]
    edge = count - 16
    chunks, _, span = total.shape

    def product(c, rows):
        part = None
        for m in range(3):
            term = nt(
                rounded[rows, m * width : (m + 1) * width], w[m, c * span : (c + 1) * span, :]
            )
            part = term if part is None else part + term
        total[c, rows] = part

    for m in range(3):
        rounded[:edge, m * width : (m + 1) * width] = raw_part(cw, grads, m, 0, edge)
    product(0, slice(0, edge))
    spill_copy.wait()
    grads[:, count:, :] = jnp.where(me == ctx - 1, jnp.zeros_like(spill), spill[...])
    for m in range(3):
        rounded[edge:, m * width : (m + 1) * width] = raw_part(cw, grads, m, edge, 16)
    product(0, slice(edge, count))
    block = count // head_axis
    sibling = head_me + 1 - 2 * (head_me % 2)
    far = (head_me + 2) % 4

    def rows_of(c, owner):
        return total[c, pl.ds(pl.multiple_of(owner * block, 16), block), :]

    near_copies, far_copies = [], []

    def pass_on(c):
        near_copies[c].wait_recv()
        far_out[c] = (rows_of(c, far) + near_in[c, block:].astype(F32)).astype(BF16)
        copy = send(
            far_out.at[c], far_in.at[c], far_send.at[c], far_recv.at[c], "head", far
        )
        copy.start()
        far_copies.append(copy)

    for c in range(chunks):
        if c > 0:
            product(c, slice(0, count))
        near_out[c, :block] = rows_of(c, sibling).astype(BF16)
        near_out[c, block:] = rows_of(c, (sibling + 2) % 4).astype(BF16)
        copy = send(
            near_out.at[c], near_in.at[c], near_send.at[c], near_recv.at[c], "head", sibling
        )
        copy.start()
        near_copies.append(copy)
        if c > 0:
            pass_on(c - 1)
    pass_on(chunks - 1)
    for copy in taps_copies:
        copy.wait()
    summed = taps[0]
    for i in range(1, ctx):
        summed = summed + taps[i]
    for m in range(3):
        taps_out[m] = summed[m * KW : (m + 1) * KW]
    for c in range(chunks):
        far_copies[c].wait_recv()
        result = rows_of(c, head_me) + near_in[c, :block].astype(F32) + far_in[c].astype(F32)
        out[:, c * span : (c + 1) * span] = result.astype(BF16)
    for copy in near_copies + far_copies + pair_copies:
        copy.wait_send()

    @pl.when(place < pairs - 1)
    def _():
        for copy in forward_copies:
            copy.wait_send()

    @pl.when(place > 0)
    def _():
        for copy in backward_copies:
            copy.wait_send()


def store_kernel(grad, taps, grad_out, taps_out):
    grad_out[...] = grad[...]
    taps_out[...] = taps[...]


def on_device(inputs, projection, conv_weight, gate_code, beta_code, grad_out):
    count, depth = inputs.shape
    heads = gate_code.shape[0]
    width = heads * DK
    ctx, head_axis = lax.axis_size("ctx"), lax.axis_size("head")
    chunks = 4
    span = depth // chunks
    block = count // head_axis
    dma = pltpu.SemaphoreType.DMA
    input_grad, taps = pl.pallas_call(
        functools.partial(whole_kernel, heads),
        out_shape=(
            jax.ShapeDtypeStruct((block, depth), BF16),
            jax.ShapeDtypeStruct((3, KW, width), F32),
        ),
        in_specs=[ANY] * 6,
        out_specs=(VMEM, VMEM),
        scratch_shapes=[
            pltpu.VMEM(inputs.shape, BF16),
            pltpu.VMEM(projection.shape, BF16),
            pltpu.VMEM(conv_weight.shape, F32),
            pltpu.VMEM(gate_code.shape, jnp.int32),
            pltpu.VMEM(beta_code.shape, jnp.int32),
            pltpu.VMEM(grad_out.shape, BF16),
            pltpu.VMEM((heads, 3, DK, DK), F32),
            pltpu.VMEM((3, count + HALO, width), F32),
            pltpu.VMEM((3, count, width), F32),
            pltpu.VMEM((3, count + 8, width), F32),
            pltpu.VMEM((HALO, depth), BF16),
            pltpu.VMEM((3, 8, width), F32),
            pltpu.VMEM((heads, 3, DK, DK), BF16),
            pltpu.VMEM((heads, 3, DK, DK), BF16),
            pltpu.VMEM((2, heads, DK, DK), BF16),
            pltpu.VMEM((2, heads, DK, DK), BF16),
            pltpu.VMEM((ctx, 16, width), F32),
            pltpu.VMEM((count, 3 * width), BF16),
            pltpu.VMEM((chunks, count, span), F32),
            pltpu.VMEM((chunks, 2 * block, span), BF16),
            pltpu.VMEM((chunks, 2 * block, span), BF16),
            pltpu.VMEM((chunks, block, span), BF16),
            pltpu.VMEM((chunks, block, span), BF16),
            dma((8,)),
            dma((2,)),
            dma((2,)),
            dma((heads, 2)),
            dma((heads, 2)),
            dma((2, heads)),
            dma((2, heads)),
            dma((ctx - 1,)),
            dma((ctx - 1,)),
            dma((chunks,)),
            dma((chunks,)),
            dma((chunks,)),
            dma((chunks,)),
        ],
        compiler_params=pltpu.CompilerParams(
            collective_id=0, has_side_effects=True, vmem_limit_bytes=56 * 1024 * 1024
        ),
    )(inputs, projection, conv_weight, gate_code, beta_code, grad_out)
    return pl.pallas_call(
        store_kernel,
        out_shape=(
            jax.ShapeDtypeStruct((block, depth), BF16),
            jax.ShapeDtypeStruct((3, KW, width), F32),
        ),
        in_specs=[VMEM, VMEM],
        out_specs=(VMEM, VMEM),
    )(input_grad, taps)


def solution(mesh):
    return jax.shard_map(
        on_device,
        mesh=mesh,
        in_specs=(
            P("ctx", None),
            P(None, None, "head"),
            P(None, None, "head"),
            P("head", "ctx"),
            P("head", "ctx"),
            P("ctx", "head"),
        ),
        out_specs=(P(("ctx", "head"), None), P(None, None, "head")),
        check_vma=False,
    )
```

```python
import functools

import jax
import jax.numpy as jnp
from jax import lax
from jax.experimental import pallas as pl
from jax.experimental.pallas import tpu as pltpu
from jax.sharding import PartitionSpec as P

DK = 128
KW = 4
GROUP = 64
HALO = 16
F32 = jnp.float32
BF16 = jnp.bfloat16
VMEM = pl.BlockSpec(memory_space=pltpu.VMEM)
ANY = pl.BlockSpec(memory_space=pl.ANY)


def contract(a, b, dims, precise):
    def one(left, right):
        return lax.dot_general(left, right, (dims, ((), ())), preferred_element_type=F32)

    if not precise:
        return one(a.astype(BF16), b.astype(BF16))
    a_high, b_high = a.astype(BF16), b.astype(BF16)
    total = one(a_high, b_high)
    if b.dtype == F32:
        total = total + one(a_high, (b - b_high.astype(F32)).astype(BF16))
    if a.dtype == F32:
        total = total + one((a - a_high.astype(F32)).astype(BF16), b_high)
    return total


def exact_nt(a, b):
    return lax.dot_general(
        a, b, (((1,), (1,)), ((), ())), precision=lax.Precision.HIGHEST, preferred_element_type=F32
    )


def nn(a, b, precise=False):
    return contract(a, b, ((1,), (0,)), precise)


def nt(a, b, precise=False):
    return contract(a, b, ((1,), (1,)), precise)


def tn(a, b, precise=False):
    return contract(a, b, ((0,), (0,)), precise)


def unit_inverses(lowers, eye, distance):
    count = eye.shape[0]
    inverses = [eye - jnp.where(distance == 1, low, 0.0) for low in lowers]
    size = 2
    while size < count:
        mask = (distance >= size) & (distance < 2 * size)
        inner = [nn(inv, jnp.where(mask, low, 0.0)) for inv, low in zip(inverses, lowers)]
        inverses = [inv - nn(mid, inv) for inv, mid in zip(inverses, inner)]
        size *= 2
    left = [eye - inv - nn(low, inv, True) for inv, low in zip(inverses, lowers)]
    return [inv + nn(inv, rest) for inv, rest in zip(inverses, left)]


def solve_down(d, rows):
    done = []
    for b, inv in enumerate(d["inv"]):
        part = rows[b * GROUP : (b + 1) * GROUP]
        if b > 0:
            part = part - nn(d["off"][b], jnp.concatenate(done, 0), True)
        done.append(nn(inv, part, True))
    return jnp.concatenate(done, 0)


def solve_up(d, rows):
    done = []
    for b in reversed(range(len(d["inv"]))):
        part = tn(d["inv"][b], rows[b * GROUP : (b + 1) * GROUP], True)
        done.insert(0, part)
        if b > 0:
            rows = rows[: b * GROUP] - tn(d["off"][b], part, True)
    return jnp.concatenate(done, 0)


def local_part(get_weights, get_tail, x_ref, w_ref, cw_ref, gate_ref, beta_ref, g_ref, ext, slope, heads):
    count = x_ref.shape[0]
    for m in (1, 0, 2):
        get_weights(m)
        ext[m, HALO:, :] = nn(x_ref[...], w_ref[m]).astype(BF16).astype(F32)
    for n in range(4, 8):
        get_weights(n)
    tail = get_tail()
    for m in range(3):
        ext[m, :HALO, :] = nn(tail, w_ref[m]).astype(BF16).astype(F32)
    rows = lax.broadcasted_iota(jnp.int32, (count, count), 0)
    cols = lax.broadcasted_iota(jnp.int32, (count, count), 1)
    eye = (rows == cols).astype(F32)
    inclusive = (rows >= cols).astype(F32)
    strict = (rows > cols).astype(F32)
    log_gate = jnp.log(1.0 - 0.001 * gate_ref[...].astype(F32) / 1023.0)
    beta_rows = beta_ref[...].astype(F32) / 1023.0
    sums_row = exact_nt(log_gate, inclusive)
    sums_col = exact_nt(inclusive, log_gate)
    beta_cols = exact_nt(eye, beta_rows)
    act = []
    for m in range(3):
        conv = cw_ref[m, 0:1, :] * ext[m, HALO - 3 : HALO - 3 + count, :]
        for j in range(1, KW):
            conv = conv + cw_ref[m, j : j + 1, :] * ext[m, HALO - 3 + j : HALO - 3 + j + count, :]
        sig = jax.nn.sigmoid(conv)
        act.append(conv * sig)
        slope[m] = conv
    out = []
    for h in range(heads):
        lanes = slice(h * DK, (h + 1) * DK)
        q_act, k_act, v = (act[m][:, lanes] for m in range(3))
        q_scale = lax.rsqrt(jnp.sum(q_act * q_act, -1, keepdims=True) + 1e-6)
        k_scale = lax.rsqrt(jnp.sum(k_act * k_act, -1, keepdims=True) + 1e-6)
        qn = q_act * q_scale
        s_col = sums_col[:, h : h + 1]
        beta = beta_cols[:, h : h + 1]
        total = s_col[count - 1 : count, :]
        d = dict(
            q=qn * DK**-0.5,
            k=k_act * k_scale,
            v=v,
            q_scale=q_scale * DK**-0.5,
            k_scale=k_scale,
            qn=qn,
            beta=beta,
            now=jnp.exp(s_col),
            rest=jnp.exp(total - s_col),
            whole=jnp.exp(total),
            g=g_ref[:, lanes],
        )
        d["s_col"], d["s_row"] = s_col, sums_row[h : h + 1, :]
        d["beta_row"] = beta_rows[h : h + 1, :]
        d["low"], d["off"] = [], []
        for b in range(count // GROUP):
            here, before = slice(b * GROUP, (b + 1) * GROUP), slice(0, b * GROUP)
            keys = d["k"][here]
            scale = jnp.exp(s_col[here] - d["s_row"][:, here]) * strict[:GROUP, :GROUP]
            d["low"].append(nt(keys, keys, True) * (scale * beta[here]))
            if b > 0:
                scale = jnp.exp(s_col[here] - d["s_row"][:, before]) * beta[here]
                d["off"].append(nt(keys, d["k"][before], True) * scale)
            else:
                d["off"].append(None)
        out.append(d)
    blocks = count // GROUP
    inverses = unit_inverses(
        [low for d in out for low in d["low"]],
        eye[:GROUP, :GROUP],
        rows[:GROUP, :GROUP] ^ cols[:GROUP, :GROUP],
    )
    for h, d in enumerate(out):
        d["inv"] = inverses[h * blocks : (h + 1) * blocks]
        d["k_rest"] = d["rest"] * d["k"]
        d["k_now"] = (d["beta"] * d["now"]) * d["k"]
        solved = solve_down(d, jnp.concatenate([d["beta"] * d["v"], d["k_now"]], 1))
        d["u0"] = solved[:, :DK]
        d["kt"] = solved[:, DK:]
        both = tn(solved, d["k_rest"], True)
        d["B"] = both[:DK]
        d["A"] = d["whole"] * eye[:DK, :DK] - both[DK:]
    return out


def adjoint_part(per_head):
    for d in per_head:
        count = d["k"].shape[0]
        rows = lax.broadcasted_iota(jnp.int32, (count, count), 0)
        cols = lax.broadcasted_iota(jnp.int32, (count, count), 1)
        d["between_t"] = jnp.where(rows <= cols, jnp.exp(d["s_row"] - d["s_col"]), 0.0)
        d["wg"] = nn(nt(d["k"], d["q"], True) * d["between_t"], d["g"], True)
        d["C"] = tn(d["g"], d["now"] * d["q"], True) - tn(d["wg"], d["kt"], True)


def prepared_part(per_head, slope):
    for m in range(3):
        sig = jax.nn.sigmoid(slope[m])
        slope[m] = sig * (1.0 + slope[m] * (1.0 - sig))
    for d in per_head:
        count = d["k"].shape[0]
        back = solve_up(d, jnp.concatenate([d["wg"], d["k_rest"]], 1))
        d["y0"], d["kt_rest"] = back[:, :DK], back[:, DK:]
        rows = lax.broadcasted_iota(jnp.int32, (count, count), 0)
        cols = lax.broadcasted_iota(jnp.int32, (count, count), 1)
        decay = jnp.exp(d["s_col"] - d["s_row"])
        d["between"] = jnp.where(rows >= cols, decay, 0.0)
        d["low_scale"] = jnp.where(rows > cols, -d["beta"] * decay, 0.0)
        d["low_scale_t"] = jnp.where(rows < cols, -d["beta_row"] * d["between_t"], 0.0)


def carried_part(per_head, slope, grads, states):
    count = grads.shape[1] - 8
    parts = [[], [], []]
    for d, (start, arriving) in zip(per_head, states):
        u = d["u0"] - nt(d["kt"], start, True)
        y = d["y0"] + nt(d["kt_rest"], arriving, True)
        keys, asks = d["k"].astype(BF16), d["q"].astype(BF16)
        u_low, y_low = u.astype(BF16), y.astype(BF16)
        start_low, arriving_low = start.astype(BF16), arriving.astype(BF16)
        low = d["low_scale"] * nt(y_low, u_low)
        low_t = d["low_scale_t"] * nt(u_low, y_low)
        seen = d["between"] * nt(d["g"], u_low)
        seen_t = d["between_t"] * nt(u_low, d["g"])
        dq = d["now"] * nn(d["g"], start_low) + nn(seen, keys)
        dk = (
            nn(low, keys)
            + nn(low_t, keys)
            + nn(seen_t, asks)
            - (d["beta"] * d["now"]) * nn(y_low, start_low)
            + d["rest"] * nn(u_low, arriving_low)
        )
        dq = d["q_scale"] * (dq - d["qn"] * jnp.sum(d["qn"] * dq, -1, keepdims=True))
        dk = d["k_scale"] * (dk - d["k"] * jnp.sum(d["k"] * dk, -1, keepdims=True))
        for m, part in enumerate((dq, dk, d["beta"] * y)):
            parts[m].append(part)
    for m in range(3):
        grads[m, :count, :] = jnp.concatenate(parts[m], 1) * slope[m]


def tap_sums(ext, grads, taps):
    count = grads.shape[1] - 8
    for m in range(3):
        dconv = grads[m, :count, :]
        for j in range(KW):
            row = m * KW + j
            taps[row : row + 1, :] = jnp.sum(
                dconv * ext[m, HALO - 3 + j : HALO - 3 + j + count, :], 0, keepdims=True
            )
    taps[3 * KW :, :] = jnp.zeros((16 - 3 * KW, taps.shape[1]), F32)


def raw_part(cw_ref, grads, m, at, count):
    raw = cw_ref[m, KW - 1 : KW, :] * grads[m, at : at + count, :]
    for j in range(KW - 1):
        first = at + KW - 1 - j
        raw = raw + cw_ref[m, j : j + 1, :] * grads[m, first : first + count, :]
    return raw.astype(BF16)


def whole_kernel(
    heads,
    x_hbm,
    w_hbm,
    cw_hbm,
    gate_hbm,
    beta_hbm,
    g_hbm,
    out,
    taps_out,
    x,
    w,
    cw,
    gate,
    beta,
    g,
    merged,
    ext,
    slope,
    grads,
    tail,
    spill,
    pair_out,
    pair_in,
    chain_out,
    chain_in,
    taps,
    rounded,
    total,
    near_out,
    near_in,
    far_out,
    far_in,
    load_sems,
    tail_sems,
    spill_sems,
    pair_send,
    pair_recv,
    chain_send,
    chain_recv,
    taps_send,
    taps_recv,
    near_send,
    near_recv,
    far_send,
    far_recv,
):
    count, depth = x.shape
    ctx, head_axis = lax.axis_size("ctx"), lax.axis_size("head")
    me, head_me = lax.axis_index("ctx"), lax.axis_index("head")
    pairs = ctx // 2
    place, odd = me // 2, me % 2

    def send(src, dst, send_sem, recv_sem, axis, target):
        return pltpu.make_async_remote_copy(
            src_ref=src,
            dst_ref=dst,
            send_sem=send_sem,
            recv_sem=recv_sem,
            device_id={axis: target},
            device_id_type=pl.DeviceIdType.MESH,
        )

    loads = [pltpu.make_async_copy(w_hbm.at[m], w.at[m], load_sems.at[m]) for m in range(3)]
    others = ((x_hbm, x), (cw_hbm, cw), (gate_hbm, gate), (beta_hbm, beta), (g_hbm, g))
    for n, (src, dst) in enumerate(others):
        loads.append(pltpu.make_async_copy(src, dst, load_sems.at[3 + n]))
    for m in (3, 1, 0, 2, 4, 5, 6, 7):
        loads[m].start()
    barrier = pltpu.get_barrier_semaphore()
    for axis, at, size in (("ctx", me, ctx), ("head", head_me, head_axis)):
        for d in range(1, size):
            pl.semaphore_signal(
                barrier,
                inc=1,
                device_id={axis: (at + d) % size},
                device_id_type=pl.DeviceIdType.MESH,
            )
    pl.semaphore_wait(barrier, ctx + head_axis - 2)

    tail_copy = send(
        x_hbm.at[count - HALO :], tail, tail_sems.at[0], tail_sems.at[1], "ctx", (me + 1) % ctx
    )
    tail_copy.start()

    def get_tail():
        tail_copy.wait()
        return jnp.where(me == 0, jnp.zeros_like(tail), tail[...])

    def get_weights(m):
        loads[m].wait()

    loads[3].wait()
    per_head = local_part(get_weights, get_tail, x, w, cw, gate, beta, g, ext, slope, heads)
    half = place < pairs // 2
    pair_copies = {
        (h, i): send(
            pair_out.at[h, i],
            pair_in.at[h, i],
            pair_send.at[h, i],
            pair_recv.at[h, i],
            "ctx",
            me + 1 - 2 * odd,
        )
        for h in range(heads)
        for i in range(3)
    }

    def start_pair(i):
        for h in range(heads):
            pair_copies[h, i].start()

    def wait_pair(i):
        for h in range(heads):
            pair_copies[h, i].wait_recv()

    for h, d in enumerate(per_head):
        pair_out[h, 0] = d["A"].astype(BF16)
        pair_out[h, 1] = d["B"].astype(BF16)
    start_pair(0)

    @pl.when(half)
    def _():
        start_pair(1)

    adjoint_part(per_head)
    for h, d in enumerate(per_head):
        pair_out[h, 2] = d["C"].astype(BF16)
    start_pair(2)

    @pl.when(place >= pairs // 2)
    def _():
        start_pair(1)

    prepared_part(per_head, slope)
    is_odd = odd == 1

    def ordered(h, name, slot):
        own, other = per_head[h][name], pair_in[h, slot].astype(F32)
        return jnp.where(is_odd, other, own), jnp.where(is_odd, own, other)

    def merge_forward():
        wait_pair(1)
        for h in range(heads):
            (_, a_late), (b_early, b_late) = ordered(h, "A", 0), ordered(h, "B", 1)
            merged[h, 1] = nn(b_early, a_late, True) + b_late

    def merge_backward():
        wait_pair(2)
        for h in range(heads):
            (a_early, _), (c_early, c_late) = ordered(h, "A", 0), ordered(h, "C", 2)
            merged[h, 2] = nt(c_late, a_early, True) + c_early

    wait_pair(0)
    for h in range(heads):
        a_early, a_late = ordered(h, "A", 0)
        merged[h, 0] = nn(a_early, a_late, True)

    forward_copies, backward_copies = [], []
    for h in range(heads):
        forward_copies.append(
            send(
                chain_out.at[0, h],
                chain_in.at[0, h],
                chain_send.at[0, h],
                chain_recv.at[0, h],
                "ctx",
                (me + 2) % ctx,
            )
        )
        backward_copies.append(
            send(
                chain_out.at[1, h],
                chain_in.at[1, h],
                chain_send.at[1, h],
                chain_recv.at[1, h],
                "ctx",
                (me + ctx - 2) % ctx,
            )
        )

    def forward():
        @pl.when(place == 0)
        def _():
            chain_in[0] = jnp.zeros_like(chain_in[0])

        for h in range(heads):

            @pl.when(place > 0)
            def _():
                forward_copies[h].wait_recv()

            @pl.when(place < pairs - 1)
            def _():
                chain_out[0, h] = (
                    nn(chain_in[0, h], merged[h, 0], True) + merged[h, 1]
                ).astype(BF16)
                forward_copies[h].start()

    def backward():
        @pl.when(place == pairs - 1)
        def _():
            chain_in[1] = jnp.zeros_like(chain_in[1])

        for h in range(heads):

            @pl.when(place < pairs - 1)
            def _():
                backward_copies[h].wait_recv()

            @pl.when(place > 0)
            def _():
                chain_out[1, h] = (
                    nt(chain_in[1, h], merged[h, 0], True) + merged[h, 2]
                ).astype(BF16)
                backward_copies[h].start()

    @pl.when(half)
    def _():
        merge_forward()
        forward()
        merge_backward()
        backward()

    @pl.when(place >= pairs // 2)
    def _():
        merge_backward()
        backward()
        merge_forward()
        forward()

    states = []
    for h in range(heads):
        start, arriving = chain_in[0, h], chain_in[1, h]
        a_early, a_late = ordered(h, "A", 0)
        b_early, _ = ordered(h, "B", 1)
        _, c_late = ordered(h, "C", 2)
        start_odd = nn(start, a_early, True) + b_early
        arriving_even = nt(arriving, a_late, True) + c_late
        states.append(
            (
                jnp.where(is_odd, start_odd, start.astype(F32)),
                jnp.where(is_odd, arriving.astype(F32), arriving_even),
            )
        )
    carried_part(per_head, slope, grads, states)
    spill_copy = send(
        grads.at[:, 0:8, :], spill, spill_sems.at[0], spill_sems.at[1], "ctx", (me + ctx - 1) % ctx
    )
    spill_copy.start()
    width = w.shape[2]
    edge = count - 16
    chunks, _, span = total.shape

    def product(c, rows):
        part = None
        for m in range(3):
            term = nt(
                rounded[rows, m * width : (m + 1) * width], w[m, c * span : (c + 1) * span, :]
            )
            part = term if part is None else part + term
        total[c, rows] = part

    for m in range(3):
        rounded[:edge, m * width : (m + 1) * width] = raw_part(cw, grads, m, 0, edge)
    early_chunks = range(min(2, chunks))
    for c in early_chunks:
        product(c, slice(0, edge))
    spill_copy.wait()
    grads[:, count:, :] = jnp.where(me == ctx - 1, jnp.zeros_like(spill), spill[...])
    for m in range(3):
        rounded[edge:, m * width : (m + 1) * width] = raw_part(cw, grads, m, edge, 16)
    for c in early_chunks:
        product(c, slice(edge, count))
    block = count // head_axis
    sibling = head_me + 1 - 2 * (head_me % 2)
    far = (head_me + 2) % 4

    def rows_of(c, owner):
        return total[c, pl.ds(pl.multiple_of(owner * block, 16), block), :]

    near_copies, far_copies = [], []

    def pass_on(c):
        near_copies[c].wait_recv()
        far_out[c] = (rows_of(c, far) + near_in[c, block:].astype(F32)).astype(BF16)
        copy = send(
            far_out.at[c], far_in.at[c], far_send.at[c], far_recv.at[c], "head", far
        )
        copy.start()
        far_copies.append(copy)

    taps_copies = [
        send(
            taps.at[me],
            taps.at[me],
            taps_send.at[d - 1],
            taps_recv.at[d - 1],
            "ctx",
            (me + d) % ctx,
        )
        for d in range(1, ctx)
    ]
    for c in range(chunks):
        if c not in early_chunks:
            product(c, slice(0, count))
        near_out[c, :block] = rows_of(c, sibling).astype(BF16)
        near_out[c, block:] = rows_of(c, (sibling + 2) % 4).astype(BF16)
        copy = send(
            near_out.at[c], near_in.at[c], near_send.at[c], near_recv.at[c], "head", sibling
        )
        copy.start()
        near_copies.append(copy)
        if c == early_chunks[-1]:
            tap_sums(ext, grads, taps.at[me])
            for copy in taps_copies:
                copy.start()
        if c > 0:
            pass_on(c - 1)
    pass_on(chunks - 1)
    for copy in taps_copies:
        copy.wait()
    summed = taps[0]
    for i in range(1, ctx):
        summed = summed + taps[i]
    for m in range(3):
        taps_out[m] = summed[m * KW : (m + 1) * KW]
    for c in range(chunks):
        far_copies[c].wait_recv()
        result = rows_of(c, head_me) + near_in[c, :block].astype(F32) + far_in[c].astype(F32)
        out[:, c * span : (c + 1) * span] = result.astype(BF16)
    for copy in near_copies + far_copies + list(pair_copies.values()):
        copy.wait_send()

    @pl.when(place < pairs - 1)
    def _():
        for copy in forward_copies:
            copy.wait_send()

    @pl.when(place > 0)
    def _():
        for copy in backward_copies:
            copy.wait_send()


def store_kernel(grad, taps, grad_out, taps_out):
    grad_out[...] = grad[...]
    taps_out[...] = taps[...]


def on_device(inputs, projection, conv_weight, gate_code, beta_code, grad_out):
    count, depth = inputs.shape
    heads = gate_code.shape[0]
    width = heads * DK
    ctx, head_axis = lax.axis_size("ctx"), lax.axis_size("head")
    chunks = 4
    span = depth // chunks
    block = count // head_axis
    dma = pltpu.SemaphoreType.DMA
    input_grad, taps = pl.pallas_call(
        functools.partial(whole_kernel, heads),
        out_shape=(
            jax.ShapeDtypeStruct((block, depth), BF16),
            jax.ShapeDtypeStruct((3, KW, width), F32),
        ),
        in_specs=[ANY] * 6,
        out_specs=(VMEM, VMEM),
        scratch_shapes=[
            pltpu.VMEM(inputs.shape, BF16),
            pltpu.VMEM(projection.shape, BF16),
            pltpu.VMEM(conv_weight.shape, F32),
            pltpu.VMEM(gate_code.shape, jnp.int32),
            pltpu.VMEM(beta_code.shape, jnp.int32),
            pltpu.VMEM(grad_out.shape, BF16),
            pltpu.VMEM((heads, 3, DK, DK), F32),
            pltpu.VMEM((3, count + HALO, width), F32),
            pltpu.VMEM((3, count, width), F32),
            pltpu.VMEM((3, count + 8, width), F32),
            pltpu.VMEM((HALO, depth), BF16),
            pltpu.VMEM((3, 8, width), F32),
            pltpu.VMEM((heads, 3, DK, DK), BF16),
            pltpu.VMEM((heads, 3, DK, DK), BF16),
            pltpu.VMEM((2, heads, DK, DK), BF16),
            pltpu.VMEM((2, heads, DK, DK), BF16),
            pltpu.VMEM((ctx, 16, width), F32),
            pltpu.VMEM((count, 3 * width), BF16),
            pltpu.VMEM((chunks, count, span), F32),
            pltpu.VMEM((chunks, 2 * block, span), BF16),
            pltpu.VMEM((chunks, 2 * block, span), BF16),
            pltpu.VMEM((chunks, block, span), BF16),
            pltpu.VMEM((chunks, block, span), BF16),
            dma((8,)),
            dma((2,)),
            dma((2,)),
            dma((heads, 3)),
            dma((heads, 3)),
            dma((2, heads)),
            dma((2, heads)),
            dma((ctx - 1,)),
            dma((ctx - 1,)),
            dma((chunks,)),
            dma((chunks,)),
            dma((chunks,)),
            dma((chunks,)),
        ],
        compiler_params=pltpu.CompilerParams(
            collective_id=0, has_side_effects=True, vmem_limit_bytes=56 * 1024 * 1024
        ),
    )(inputs, projection, conv_weight, gate_code, beta_code, grad_out)
    return pl.pallas_call(
        store_kernel,
        out_shape=(
            jax.ShapeDtypeStruct((block, depth), BF16),
            jax.ShapeDtypeStruct((3, KW, width), F32),
        ),
        in_specs=[VMEM, VMEM],
        out_specs=(VMEM, VMEM),
    )(input_grad, taps)


def solution(mesh):
    return jax.shard_map(
        on_device,
        mesh=mesh,
        in_specs=(
            P("ctx", None),
            P(None, None, "head"),
            P(None, None, "head"),
            P("head", "ctx"),
            P("head", "ctx"),
            P("ctx", "head"),
        ),
        out_specs=(P(("ctx", "head"), None), P(None, None, "head")),
        check_vma=False,
    )
```

```python
import functools

import jax
import jax.numpy as jnp
from jax import lax
from jax.experimental import pallas as pl
from jax.experimental.pallas import tpu as pltpu
from jax.sharding import PartitionSpec as P

DK = 128
KW = 4
GROUP = 64
HALO = 16
F32 = jnp.float32
BF16 = jnp.bfloat16
VMEM = pl.BlockSpec(memory_space=pltpu.VMEM)
ANY = pl.BlockSpec(memory_space=pl.ANY)


def contract(a, b, dims, precise):
    def one(left, right):
        return lax.dot_general(left, right, (dims, ((), ())), preferred_element_type=F32)

    if not precise:
        return one(a.astype(BF16), b.astype(BF16))
    a_high, b_high = a.astype(BF16), b.astype(BF16)
    total = one(a_high, b_high)
    if b.dtype == F32:
        total = total + one(a_high, (b - b_high.astype(F32)).astype(BF16))
    if a.dtype == F32:
        total = total + one((a - a_high.astype(F32)).astype(BF16), b_high)
    return total


def exact_nt(a, b):
    return lax.dot_general(
        a, b, (((1,), (1,)), ((), ())), precision=lax.Precision.HIGHEST, preferred_element_type=F32
    )


def nn(a, b, precise=False):
    return contract(a, b, ((1,), (0,)), precise)


def nt(a, b, precise=False):
    return contract(a, b, ((1,), (1,)), precise)


def tn(a, b, precise=False):
    return contract(a, b, ((0,), (0,)), precise)


def unit_inverses(lowers, eye, distance):
    count = eye.shape[0]
    inverses = [eye - jnp.where(distance == 1, low, 0.0) for low in lowers]
    size = 2
    while size < count:
        mask = (distance >= size) & (distance < 2 * size)
        inner = [nn(inv, jnp.where(mask, low, 0.0)) for inv, low in zip(inverses, lowers)]
        inverses = [inv - nn(mid, inv) for inv, mid in zip(inverses, inner)]
        size *= 2
    left = [eye - inv - nn(low, inv, True) for inv, low in zip(inverses, lowers)]
    return [inv + nn(inv, rest) for inv, rest in zip(inverses, left)]


def solve_down(d, rows):
    done = []
    for b, inv in enumerate(d["inv"]):
        part = rows[b * GROUP : (b + 1) * GROUP]
        if b > 0:
            part = part - nn(d["off"][b], jnp.concatenate(done, 0), True)
        done.append(nn(inv, part, True))
    return jnp.concatenate(done, 0)


def solve_up(d, rows):
    done = []
    for b in reversed(range(len(d["inv"]))):
        part = tn(d["inv"][b], rows[b * GROUP : (b + 1) * GROUP], True)
        done.insert(0, part)
        if b > 0:
            rows = rows[: b * GROUP] - tn(d["off"][b], part, True)
    return jnp.concatenate(done, 0)


def local_part(get_weights, get_tail, x_ref, w_ref, cw_ref, gate_ref, beta_ref, g_ref, ext, slope, heads):
    count = x_ref.shape[0]
    for m in (1, 0, 2):
        get_weights(m)
        ext[m, HALO:, :] = nn(x_ref[...], w_ref[m]).astype(BF16).astype(F32)
    for n in range(4, 8):
        get_weights(n)
    tail = get_tail()
    for m in range(3):
        ext[m, :HALO, :] = nn(tail, w_ref[m]).astype(BF16).astype(F32)
    rows = lax.broadcasted_iota(jnp.int32, (count, count), 0)
    cols = lax.broadcasted_iota(jnp.int32, (count, count), 1)
    eye = (rows == cols).astype(F32)
    inclusive = (rows >= cols).astype(F32)
    strict = (rows > cols).astype(F32)
    log_gate = jnp.log(1.0 - 0.001 * gate_ref[...].astype(F32) / 1023.0)
    beta_rows = beta_ref[...].astype(F32) / 1023.0
    sums_row = exact_nt(log_gate, inclusive)
    sums_col = exact_nt(inclusive, log_gate)
    beta_cols = exact_nt(eye, beta_rows)
    act = []
    for m in range(3):
        conv = cw_ref[m, 0:1, :] * ext[m, HALO - 3 : HALO - 3 + count, :]
        for j in range(1, KW):
            conv = conv + cw_ref[m, j : j + 1, :] * ext[m, HALO - 3 + j : HALO - 3 + j + count, :]
        sig = jax.nn.sigmoid(conv)
        act.append(conv * sig)
        slope[m] = conv
    out = []
    for h in range(heads):
        lanes = slice(h * DK, (h + 1) * DK)
        q_act, k_act, v = (act[m][:, lanes] for m in range(3))
        q_scale = lax.rsqrt(jnp.sum(q_act * q_act, -1, keepdims=True) + 1e-6)
        k_scale = lax.rsqrt(jnp.sum(k_act * k_act, -1, keepdims=True) + 1e-6)
        qn = q_act * q_scale
        s_col = sums_col[:, h : h + 1]
        beta = beta_cols[:, h : h + 1]
        total = s_col[count - 1 : count, :]
        d = dict(
            q=qn * DK**-0.5,
            k=k_act * k_scale,
            v=v,
            q_scale=q_scale * DK**-0.5,
            k_scale=k_scale,
            qn=qn,
            beta=beta,
            now=jnp.exp(s_col),
            rest=jnp.exp(total - s_col),
            whole=jnp.exp(total),
            g=g_ref[:, lanes],
        )
        d["s_col"], d["s_row"] = s_col, sums_row[h : h + 1, :]
        d["beta_row"] = beta_rows[h : h + 1, :]
        d["low"], d["off"] = [], []
        for b in range(count // GROUP):
            here, before = slice(b * GROUP, (b + 1) * GROUP), slice(0, b * GROUP)
            keys = d["k"][here]
            scale = jnp.exp(s_col[here] - d["s_row"][:, here]) * strict[:GROUP, :GROUP]
            d["low"].append(nt(keys, keys, True) * (scale * beta[here]))
            if b > 0:
                scale = jnp.exp(s_col[here] - d["s_row"][:, before]) * beta[here]
                d["off"].append(nt(keys, d["k"][before], True) * scale)
            else:
                d["off"].append(None)
        out.append(d)
    blocks = count // GROUP
    inverses = unit_inverses(
        [low for d in out for low in d["low"]],
        eye[:GROUP, :GROUP],
        rows[:GROUP, :GROUP] ^ cols[:GROUP, :GROUP],
    )
    for h, d in enumerate(out):
        d["inv"] = inverses[h * blocks : (h + 1) * blocks]
        d["k_rest"] = d["rest"] * d["k"]
        d["k_now"] = (d["beta"] * d["now"]) * d["k"]
        solved = solve_down(d, jnp.concatenate([d["beta"] * d["v"], d["k_now"]], 1))
        d["u0"] = solved[:, :DK]
        d["kt"] = solved[:, DK:]
        both = tn(solved, d["k_rest"], True)
        d["B"] = both[:DK]
        d["A"] = d["whole"] * eye[:DK, :DK] - both[DK:]
    return out


def adjoint_part(per_head):
    for d in per_head:
        count = d["k"].shape[0]
        rows = lax.broadcasted_iota(jnp.int32, (count, count), 0)
        cols = lax.broadcasted_iota(jnp.int32, (count, count), 1)
        d["between_t"] = jnp.where(rows <= cols, jnp.exp(d["s_row"] - d["s_col"]), 0.0)
        d["wg"] = nn(nt(d["k"], d["q"], True) * d["between_t"], d["g"], True)
        d["C"] = tn(d["g"], d["now"] * d["q"], True) - tn(d["wg"], d["kt"], True)


def prepared_part(per_head, slope):
    for m in range(3):
        sig = jax.nn.sigmoid(slope[m])
        slope[m] = sig * (1.0 + slope[m] * (1.0 - sig))
    for d in per_head:
        count = d["k"].shape[0]
        back = solve_up(d, jnp.concatenate([d["wg"], d["k_rest"]], 1))
        d["y0"], d["kt_rest"] = back[:, :DK], back[:, DK:]
        rows = lax.broadcasted_iota(jnp.int32, (count, count), 0)
        cols = lax.broadcasted_iota(jnp.int32, (count, count), 1)
        decay = jnp.exp(d["s_col"] - d["s_row"])
        d["between"] = jnp.where(rows >= cols, decay, 0.0)
        d["low_scale"] = jnp.where(rows > cols, -d["beta"] * decay, 0.0)
        d["low_scale_t"] = jnp.where(rows < cols, -d["beta_row"] * d["between_t"], 0.0)


def carried_part(per_head, slope, grads, states):
    count = grads.shape[1] - 8
    parts = [[], [], []]
    for d, (start, arriving) in zip(per_head, states):
        u = d["u0"] - nt(d["kt"], start, True)
        y = d["y0"] + nt(d["kt_rest"], arriving, True)
        keys, asks = d["k"].astype(BF16), d["q"].astype(BF16)
        u_low, y_low = u.astype(BF16), y.astype(BF16)
        start_low, arriving_low = start.astype(BF16), arriving.astype(BF16)
        low = d["low_scale"] * nt(y_low, u_low)
        low_t = d["low_scale_t"] * nt(u_low, y_low)
        seen = d["between"] * nt(d["g"], u_low)
        seen_t = d["between_t"] * nt(u_low, d["g"])
        dq = d["now"] * nn(d["g"], start_low) + nn(seen, keys)
        dk = (
            nn(low, keys)
            + nn(low_t, keys)
            + nn(seen_t, asks)
            - (d["beta"] * d["now"]) * nn(y_low, start_low)
            + d["rest"] * nn(u_low, arriving_low)
        )
        dq = d["q_scale"] * (dq - d["qn"] * jnp.sum(d["qn"] * dq, -1, keepdims=True))
        dk = d["k_scale"] * (dk - d["k"] * jnp.sum(d["k"] * dk, -1, keepdims=True))
        for m, part in enumerate((dq, dk, d["beta"] * y)):
            parts[m].append(part)
    for m in range(3):
        grads[m, :count, :] = jnp.concatenate(parts[m], 1) * slope[m]


def tap_sums(ext, grads, taps):
    count = grads.shape[1] - 8
    for m in range(3):
        dconv = grads[m, :count, :]
        for j in range(KW):
            row = m * KW + j
            taps[row : row + 1, :] = jnp.sum(
                dconv * ext[m, HALO - 3 + j : HALO - 3 + j + count, :], 0, keepdims=True
            )
    taps[3 * KW :, :] = jnp.zeros((16 - 3 * KW, taps.shape[1]), F32)


def raw_part(cw_ref, grads, m, at, count):
    raw = cw_ref[m, KW - 1 : KW, :] * grads[m, at : at + count, :]
    for j in range(KW - 1):
        first = at + KW - 1 - j
        raw = raw + cw_ref[m, j : j + 1, :] * grads[m, first : first + count, :]
    return raw.astype(BF16)


def whole_kernel(
    heads,
    x_hbm,
    w_hbm,
    cw_hbm,
    gate_hbm,
    beta_hbm,
    g_hbm,
    out,
    taps_out,
    x,
    w,
    cw,
    gate,
    beta,
    g,
    merged,
    ext,
    slope,
    grads,
    tail,
    spill,
    pair_out,
    pair_in,
    chain_out,
    chain_in,
    taps,
    rounded,
    total,
    near_out,
    near_in,
    far_out,
    far_in,
    load_sems,
    tail_sems,
    spill_sems,
    pair_send,
    pair_recv,
    chain_send,
    chain_recv,
    taps_send,
    taps_recv,
    near_send,
    near_recv,
    far_send,
    far_recv,
):
    count, depth = x.shape
    ctx, head_axis = lax.axis_size("ctx"), lax.axis_size("head")
    me, head_me = lax.axis_index("ctx"), lax.axis_index("head")
    pairs = ctx // 2
    place, odd = me // 2, me % 2

    def send(src, dst, send_sem, recv_sem, axis, target):
        return pltpu.make_async_remote_copy(
            src_ref=src,
            dst_ref=dst,
            send_sem=send_sem,
            recv_sem=recv_sem,
            device_id={axis: target},
            device_id_type=pl.DeviceIdType.MESH,
        )

    loads = [pltpu.make_async_copy(w_hbm.at[m], w.at[m], load_sems.at[m]) for m in range(3)]
    others = ((x_hbm, x), (cw_hbm, cw), (gate_hbm, gate), (beta_hbm, beta), (g_hbm, g))
    for n, (src, dst) in enumerate(others):
        loads.append(pltpu.make_async_copy(src, dst, load_sems.at[3 + n]))
    for m in (3, 1, 0, 2, 4, 5, 6, 7):
        loads[m].start()
    barrier = pltpu.get_barrier_semaphore()
    for axis, at, size in (("ctx", me, ctx), ("head", head_me, head_axis)):
        for d in range(1, size):
            pl.semaphore_signal(
                barrier,
                inc=1,
                device_id={axis: (at + d) % size},
                device_id_type=pl.DeviceIdType.MESH,
            )
    pl.semaphore_wait(barrier, ctx + head_axis - 2)

    tail_copy = send(
        x_hbm.at[count - HALO :], tail, tail_sems.at[0], tail_sems.at[1], "ctx", (me + 1) % ctx
    )
    tail_copy.start()

    def get_tail():
        tail_copy.wait()
        return jnp.where(me == 0, jnp.zeros_like(tail), tail[...])

    def get_weights(m):
        loads[m].wait()

    loads[3].wait()
    per_head = local_part(get_weights, get_tail, x, w, cw, gate, beta, g, ext, slope, heads)
    half = place < pairs // 2
    pair_copies = {
        (h, i): send(
            pair_out.at[h, i],
            pair_in.at[h, i],
            pair_send.at[h, i],
            pair_recv.at[h, i],
            "ctx",
            me + 1 - 2 * odd,
        )
        for h in range(heads)
        for i in range(3)
    }

    def start_pair(i):
        for h in range(heads):
            pair_copies[h, i].start()

    def wait_pair(i):
        for h in range(heads):
            pair_copies[h, i].wait_recv()

    for h, d in enumerate(per_head):
        pair_out[h, 0] = d["A"].astype(BF16)
        pair_out[h, 1] = d["B"].astype(BF16)
    start_pair(0)

    @pl.when(half)
    def _():
        start_pair(1)

    adjoint_part(per_head)
    for h, d in enumerate(per_head):
        pair_out[h, 2] = d["C"].astype(BF16)
    start_pair(2)

    @pl.when(place >= pairs // 2)
    def _():
        start_pair(1)

    prepared_part(per_head, slope)
    is_odd = odd == 1

    def ordered(h, name, slot):
        own, other = per_head[h][name], pair_in[h, slot].astype(F32)
        return jnp.where(is_odd, other, own), jnp.where(is_odd, own, other)

    def merge_forward():
        wait_pair(1)
        for h in range(heads):
            (_, a_late), (b_early, b_late) = ordered(h, "A", 0), ordered(h, "B", 1)
            merged[h, 1] = nn(b_early, a_late, True) + b_late

    def merge_backward():
        wait_pair(2)
        for h in range(heads):
            (a_early, _), (c_early, c_late) = ordered(h, "A", 0), ordered(h, "C", 2)
            merged[h, 2] = nt(c_late, a_early, True) + c_early

    wait_pair(0)
    for h in range(heads):
        a_early, a_late = ordered(h, "A", 0)
        merged[h, 0] = nn(a_early, a_late, True)

    forward_copies, backward_copies = [], []
    for h in range(heads):
        forward_copies.append(
            send(
                chain_out.at[0, h],
                chain_in.at[0, h],
                chain_send.at[0, h],
                chain_recv.at[0, h],
                "ctx",
                (me + 2) % ctx,
            )
        )
        backward_copies.append(
            send(
                chain_out.at[1, h],
                chain_in.at[1, h],
                chain_send.at[1, h],
                chain_recv.at[1, h],
                "ctx",
                (me + ctx - 2) % ctx,
            )
        )

    def forward():
        @pl.when(place == 0)
        def _():
            chain_in[0] = jnp.zeros_like(chain_in[0])

        for h in range(heads):

            @pl.when(place > 0)
            def _():
                forward_copies[h].wait_recv()

            @pl.when(place < pairs - 1)
            def _():
                chain_out[0, h] = (
                    nn(chain_in[0, h], merged[h, 0], True) + merged[h, 1]
                ).astype(BF16)
                forward_copies[h].start()

    def backward():
        @pl.when(place == pairs - 1)
        def _():
            chain_in[1] = jnp.zeros_like(chain_in[1])

        for h in range(heads):

            @pl.when(place < pairs - 1)
            def _():
                backward_copies[h].wait_recv()

            @pl.when(place > 0)
            def _():
                chain_out[1, h] = (
                    nt(chain_in[1, h], merged[h, 0], True) + merged[h, 2]
                ).astype(BF16)
                backward_copies[h].start()

    @pl.when(half)
    def _():
        merge_forward()
        forward()
        merge_backward()
        backward()

    @pl.when(place >= pairs // 2)
    def _():
        merge_backward()
        backward()
        merge_forward()
        forward()

    states = []
    for h in range(heads):
        start, arriving = chain_in[0, h], chain_in[1, h]
        a_early, a_late = ordered(h, "A", 0)
        b_early, _ = ordered(h, "B", 1)
        _, c_late = ordered(h, "C", 2)
        start_odd = nn(start, a_early, True) + b_early
        arriving_even = nt(arriving, a_late, True) + c_late
        states.append(
            (
                jnp.where(is_odd, start_odd, start.astype(F32)),
                jnp.where(is_odd, arriving.astype(F32), arriving_even),
            )
        )
    carried_part(per_head, slope, grads, states)
    spill_copy = send(
        grads.at[:, 0:8, :], spill, spill_sems.at[0], spill_sems.at[1], "ctx", (me + ctx - 1) % ctx
    )
    spill_copy.start()
    width = w.shape[2]
    edge = count - 16
    chunks, _, span = total.shape

    def product(c, rows):
        part = None
        for m in range(3):
            term = nt(
                rounded[rows, m * width : (m + 1) * width], w[m, c * span : (c + 1) * span, :]
            )
            part = term if part is None else part + term
        total[c, rows] = part

    for m in range(3):
        rounded[:edge, m * width : (m + 1) * width] = raw_part(cw, grads, m, 0, edge)
    early_chunks = range(min(4, chunks))
    for c in early_chunks:
        product(c, slice(0, edge))
    spill_copy.wait()
    grads[:, count:, :] = jnp.where(me == ctx - 1, jnp.zeros_like(spill), spill[...])
    for m in range(3):
        rounded[edge:, m * width : (m + 1) * width] = raw_part(cw, grads, m, edge, 16)
    for c in early_chunks:
        product(c, slice(edge, count))
    block = count // head_axis
    sibling = head_me + 1 - 2 * (head_me % 2)
    far = (head_me + 2) % 4

    def rows_of(c, owner):
        return total[c, pl.ds(pl.multiple_of(owner * block, 16), block), :]

    near_copies, far_copies = [], []

    def pass_on(c):
        near_copies[c].wait_recv()
        far_out[c] = (rows_of(c, far) + near_in[c, block:].astype(F32)).astype(BF16)
        copy = send(
            far_out.at[c], far_in.at[c], far_send.at[c], far_recv.at[c], "head", far
        )
        copy.start()
        far_copies.append(copy)

    taps_copies = [
        send(
            taps.at[me],
            taps.at[me],
            taps_send.at[d - 1],
            taps_recv.at[d - 1],
            "ctx",
            (me + d) % ctx,
        )
        for d in range(1, ctx)
    ]
    for c in range(chunks):
        if c not in early_chunks:
            product(c, slice(0, count))
        near_out[c, :block] = rows_of(c, sibling).astype(BF16)
        near_out[c, block:] = rows_of(c, (sibling + 2) % 4).astype(BF16)
        copy = send(
            near_out.at[c], near_in.at[c], near_send.at[c], near_recv.at[c], "head", sibling
        )
        copy.start()
        near_copies.append(copy)
        if c == 1:
            tap_sums(ext, grads, taps.at[me])
            for copy in taps_copies:
                copy.start()
        if c > 0:
            pass_on(c - 1)
    pass_on(chunks - 1)
    for copy in taps_copies:
        copy.wait()
    summed = taps[0]
    for i in range(1, ctx):
        summed = summed + taps[i]
    for m in range(3):
        taps_out[m] = summed[m * KW : (m + 1) * KW]
    for c in range(chunks):
        far_copies[c].wait_recv()
        result = rows_of(c, head_me) + near_in[c, :block].astype(F32) + far_in[c].astype(F32)
        out[:, c * span : (c + 1) * span] = result.astype(BF16)
    for copy in near_copies + far_copies + list(pair_copies.values()):
        copy.wait_send()

    @pl.when(place < pairs - 1)
    def _():
        for copy in forward_copies:
            copy.wait_send()

    @pl.when(place > 0)
    def _():
        for copy in backward_copies:
            copy.wait_send()


def store_kernel(grad, taps, grad_out, taps_out):
    grad_out[...] = grad[...]
    taps_out[...] = taps[...]


def on_device(inputs, projection, conv_weight, gate_code, beta_code, grad_out):
    count, depth = inputs.shape
    heads = gate_code.shape[0]
    width = heads * DK
    ctx, head_axis = lax.axis_size("ctx"), lax.axis_size("head")
    chunks = 8
    span = depth // chunks
    block = count // head_axis
    dma = pltpu.SemaphoreType.DMA
    input_grad, taps = pl.pallas_call(
        functools.partial(whole_kernel, heads),
        out_shape=(
            jax.ShapeDtypeStruct((block, depth), BF16),
            jax.ShapeDtypeStruct((3, KW, width), F32),
        ),
        in_specs=[ANY] * 6,
        out_specs=(VMEM, VMEM),
        scratch_shapes=[
            pltpu.VMEM(inputs.shape, BF16),
            pltpu.VMEM(projection.shape, BF16),
            pltpu.VMEM(conv_weight.shape, F32),
            pltpu.VMEM(gate_code.shape, jnp.int32),
            pltpu.VMEM(beta_code.shape, jnp.int32),
            pltpu.VMEM(grad_out.shape, BF16),
            pltpu.VMEM((heads, 3, DK, DK), F32),
            pltpu.VMEM((3, count + HALO, width), F32),
            pltpu.VMEM((3, count, width), F32),
            pltpu.VMEM((3, count + 8, width), F32),
            pltpu.VMEM((HALO, depth), BF16),
            pltpu.VMEM((3, 8, width), F32),
            pltpu.VMEM((heads, 3, DK, DK), BF16),
            pltpu.VMEM((heads, 3, DK, DK), BF16),
            pltpu.VMEM((2, heads, DK, DK), BF16),
            pltpu.VMEM((2, heads, DK, DK), BF16),
            pltpu.VMEM((ctx, 16, width), F32),
            pltpu.VMEM((count, 3 * width), BF16),
            pltpu.VMEM((chunks, count, span), F32),
            pltpu.VMEM((chunks, 2 * block, span), BF16),
            pltpu.VMEM((chunks, 2 * block, span), BF16),
            pltpu.VMEM((chunks, block, span), BF16),
            pltpu.VMEM((chunks, block, span), BF16),
            dma((8,)),
            dma((2,)),
            dma((2,)),
            dma((heads, 3)),
            dma((heads, 3)),
            dma((2, heads)),
            dma((2, heads)),
            dma((ctx - 1,)),
            dma((ctx - 1,)),
            dma((chunks,)),
            dma((chunks,)),
            dma((chunks,)),
            dma((chunks,)),
        ],
        compiler_params=pltpu.CompilerParams(
            collective_id=0, has_side_effects=True, vmem_limit_bytes=56 * 1024 * 1024
        ),
    )(inputs, projection, conv_weight, gate_code, beta_code, grad_out)
    return pl.pallas_call(
        store_kernel,
        out_shape=(
            jax.ShapeDtypeStruct((block, depth), BF16),
            jax.ShapeDtypeStruct((3, KW, width), F32),
        ),
        in_specs=[VMEM, VMEM],
        out_specs=(VMEM, VMEM),
    )(input_grad, taps)


def solution(mesh):
    return jax.shard_map(
        on_device,
        mesh=mesh,
        in_specs=(
            P("ctx", None),
            P(None, None, "head"),
            P(None, None, "head"),
            P("head", "ctx"),
            P("head", "ctx"),
            P("ctx", "head"),
        ),
        out_specs=(P(("ctx", "head"), None), P(None, None, "head")),
        check_vma=False,
    )
```
